512 devices in a mesh: fe: 64 (over z, y), band: 8 (over x, core).
Axes of the slice: x: 4, y: 4, z: 16, core: 2. Of those that a mesh axis runs over, the one named last changes fastest.
Arguments:
- wavefunctions: float32 [128, 65536], P('band', 'fe'), may hold values from -11 to 11
- potential: float32 [65536], P('fe'), may hold values from -0.3 to 0.6
- element_matrix: float32 [512, 512], replicated, may hold values from -0.1 to 0.6, as said below
- projectors: float32 [256, 18, 512], P('fe'), may hold values from -0.078125 to 0.078125
- coupling: float32 [512, 18], replicated, may hold values from 0.1 to 0.8
- connectivity: int32 [256, 512], P('fe'), may hold values from 0 to 1279, as said below
- send_list: int32 [16384], P('fe'), may hold values from 0 to 1023, as said below
- atom_of_cell: int32 [256], P('fe'), may hold values from 0 to 15, as said below
Outputs:
- filtered: float32 [128, 65536], P('band', 'fe')
- projected: float32 [128, 128], P(None, 'band')
- correlation: float32 [128, 128], P(None, 'band')
The draws below stay inside these ranges and needn't reach their ends.
Inputs may be any that keep to these rules, and one draw needn't show every extreme that they name: `connectivity`: entries below 1024 name owned nodes, the others ghost slots; only the last cell of each fe index names ghost slots; each ghost slot appears exactly once among one fe index's cells, each owned node once or twice. `send_list`: the 256 entries of one fe index are distinct. `atom_of_cell`: the last cell of each fe index names slots of 8 or more. `element_matrix`: Symmetric.
All inputs are finite; a program needn't handle non-finite values.
Results may differ from the reference program's by a relative error of at most 0.00016.
Values sent between devices are 32-bit elements; how exact they have to be, the bound alone decides.
No kernel may reach another device: no remote copies, remote signals or barrier semaphores. Data moves between devices by JAX's collectives and lax.ppermute only.
A program may use at most 64 MiB of HBM per device.

```python
import math
import jax
import jax.numpy as jnp
from jax import lax

W = 128
NPC = 512
NPROJ = 18
DEGREE = 6
NODE_DEV = 1024
ATOM_DEV = 8
GHOST = 256
CELL_DEV = 4
NODES = 65536
ATOMS = 512
N_FE = 64


def draw_wavefunctions(key, part):
    key = jax.random.fold_in(key, 5)
    node_ramp = 0.6 + 1.2 * jnp.arange(NODES, dtype=jnp.float32) / NODES
    samples = jnp.clip(jax.random.normal(key, (W, NODES), jnp.float32), -5.0, 5.0)
    values = samples * node_ramp[None, :]
    return values.astype(jnp.float32)


def draw_element_matrix(key, part):
    key = jax.random.fold_in(key, 7)
    key_one, key_two = jax.random.split(key)
    diagonal = jax.random.uniform(key_one, (NPC,), jnp.float32, 0.2, 0.5)
    spread = 0.07 / NPC ** 0.5
    offdiag = spread * jnp.clip(jax.random.normal(key_two, (NPC, NPC), jnp.float32), -4.0, 4.0)
    symmetric = (offdiag + offdiag.T) * 0.7071
    return (symmetric + jnp.diag(diagonal)).astype(jnp.float32)


def draw_connectivity(key, part):
    key = jax.random.fold_in(key, 11)

    def per_device(subkey):
        key_one, key_two, key_three = jax.random.split(subkey, 3)
        owned_ids = jnp.arange(NODE_DEV, dtype=jnp.int32)
        repeats = jax.random.permutation(key_one, NODE_DEV)[:3 * NODE_DEV // 4].astype(jnp.int32)
        ref_pool = jax.random.permutation(key_two, jnp.concatenate([owned_ids, repeats]))
        inner_refs = ref_pool[:(CELL_DEV - CELL_DEV // 4) * NPC]
        edge_owned = ref_pool[(CELL_DEV - CELL_DEV // 4) * NPC:]
        ghost_ids = NODE_DEV + jnp.arange(GHOST, dtype=jnp.int32)
        edge_refs = jax.random.permutation(key_three, jnp.concatenate([edge_owned, ghost_ids]))
        return jnp.concatenate([inner_refs, edge_refs]).astype(jnp.int32).reshape(CELL_DEV, NPC)
    subkeys = jax.random.split(key, N_FE)
    return jax.vmap(per_device)(subkeys).reshape(N_FE * CELL_DEV, NPC)


def draw_send_list(key, part):
    key = jax.random.fold_in(key, 13)

    def per_device(subkey):
        middle = 1 + jax.random.permutation(subkey, NODE_DEV - 2)[:GHOST - 2].astype(jnp.int32)
        chosen = jnp.concatenate([jnp.array([0, NODE_DEV - 1], dtype=jnp.int32), middle])
        return jax.random.permutation(jax.random.fold_in(subkey, 1), chosen).astype(jnp.int32)
    subkeys = jax.random.split(key, N_FE)
    return jax.vmap(per_device)(subkeys).reshape(N_FE * GHOST)


def draw_atom_of_cell(key, part):
    key = jax.random.fold_in(key, 17)

    def per_device(subkey):
        key_one, key_two = jax.random.split(subkey)
        inner = jax.random.randint(key_one, (CELL_DEV - CELL_DEV // 4,), 0, 2 * ATOM_DEV).astype(jnp.int32)
        edge = jax.random.randint(key_two, (CELL_DEV // 4,), ATOM_DEV, 2 * ATOM_DEV).astype(jnp.int32)
        inner = inner.at[0].set(0)
        edge = edge.at[CELL_DEV // 4 - 1].set(2 * ATOM_DEV - 1)
        return jnp.concatenate([inner, edge]).astype(jnp.int32)
    subkeys = jax.random.split(key, N_FE)
    return jax.vmap(per_device)(subkeys).reshape(N_FE * CELL_DEV)


def steps_of(key, extent, pieces, least, high):
    factor_of, own = 1.0, jax.random.fold_in(key, 6)
    for dim, parts in pieces:
        draws = jnp.exp(jax.random.uniform(jax.random.fold_in(own, dim), (parts,), jnp.float32, least / len(pieces), high / len(pieces)))
        factor_of = factor_of * jnp.repeat(draws, extent[dim] // parts).reshape([-1 if axis == dim else 1 for axis in range(len(extent))])
    return factor_of


def centred(stream_key, dims, scale, reach, shards=(), held_as=jnp.bfloat16):
    values = scale * jax.random.normal(stream_key, dims, jnp.float32)
    if shards:
        values = values * steps_of(stream_key, dims, shards, -0.22, 0.18)
    return jnp.clip(values, -reach, reach).astype(held_as)


def setup_inputs(seed: int = 0) -> dict:
    key_of = jax.random.split(jax.random.key(seed), 9)
    wavefunctions = draw_wavefunctions(jax.random.fold_in(key_of[8], 71), 0)
    potential = jnp.clip(-0.3 + 0.90000004 * jax.random.uniform(key_of[1], (NODES,), jnp.float32) ** steps_of(key_of[1], (NODES,), ((0, 64),), -0.2, 0.2), -0.3, 0.6)
    element_matrix = draw_element_matrix(jax.random.fold_in(key_of[8], 71), 0)
    projectors = centred(key_of[3], (N_FE * CELL_DEV, NPROJ, NPC), (1 / (8 * NPC) ** 0.5), 0.078125, ((0, 64),), jnp.float32)
    coupling = jnp.clip(jnp.exp(jax.random.uniform(key_of[4], (ATOMS, NPROJ), jnp.float32, math.log(0.1), math.log(0.8))), 0.1, 0.8)
    connectivity = draw_connectivity(jax.random.fold_in(key_of[8], 71), 0)
    send_list = draw_send_list(jax.random.fold_in(key_of[8], 71), 0)
    atom_of_cell = draw_atom_of_cell(jax.random.fold_in(key_of[8], 71), 0)
    return {"wavefunctions": wavefunctions, "potential": potential, "element_matrix": element_matrix, "projectors": projectors, "coupling": coupling, "connectivity": connectivity, "send_list": send_list, "atom_of_cell": atom_of_cell}


PRECISE = lax.Precision.HIGHEST
CENTER = 0.9
HALF_WIDTH = 1.1


def global_maps(connectivity, send_list, atom_of_cell):
    device = jnp.arange(N_FE * CELL_DEV, dtype=jnp.int32) // CELL_DEV
    upper = (device + 1) % N_FE
    lower = (device + N_FE - 1) % N_FE
    ghost_slot = jnp.clip(connectivity - NODE_DEV, 0, GHOST - 1).astype(jnp.int32)
    ghost_node = send_list[upper[:, None] * GHOST + ghost_slot]
    node_ids = jnp.where(connectivity < NODE_DEV, device[:, None] * NODE_DEV + connectivity, upper[:, None] * NODE_DEV + ghost_node)
    atom_ids = jnp.where(atom_of_cell < ATOM_DEV, lower * ATOM_DEV + atom_of_cell, device * ATOM_DEV + atom_of_cell - ATOM_DEV)
    return node_ids.astype(jnp.int32), atom_ids.astype(jnp.int32)


def apply_hamiltonian(vectors, node_ids, atom_ids, element_matrix, projectors, coupling, potential):
    block_data = (node_ids.reshape(N_FE, CELL_DEV, NPC), atom_ids.reshape(N_FE, CELL_DEV), projectors.reshape(N_FE, CELL_DEV, NPROJ, NPC))

    def project(running, block_item):
        cell_ids, cell_atoms, proj_block = block_item
        cell_rows = vectors[:, cell_ids]
        partial_value = jnp.einsum("wcn,cpn->wcp", cell_rows, proj_block, precision=PRECISE)
        return running.at[:, cell_atoms, :].add(partial_value), None

    start_sums = jnp.zeros((vectors.shape[0], ATOMS, NPROJ), vectors.dtype)
    atom_sums, unused = lax.scan(project, start_sums, block_data)
    weights = atom_sums * coupling[None, :, :]

    def assemble(running, block_item):
        cell_ids, cell_atoms, proj_block = block_item
        cell_rows = vectors[:, cell_ids]
        stiffness = jnp.einsum("wcn,nm->wcm", cell_rows, element_matrix, precision=PRECISE)
        nonlocal_part = jnp.einsum("wcp,cpn->wcn", weights[:, cell_atoms, :], proj_block, precision=PRECISE)
        return running.at[:, cell_ids].add(stiffness + nonlocal_part), None

    assembled, unused = lax.scan(assemble, jnp.zeros_like(vectors), block_data)
    return assembled + potential[None, :] * vectors


def reference(wavefunctions, potential, element_matrix, projectors, coupling, connectivity, send_list, atom_of_cell):
    node_ids, atom_ids = global_maps(connectivity, send_list, atom_of_cell)

    def hamiltonian(vectors):
        return apply_hamiltonian(vectors, node_ids, atom_ids, element_matrix, projectors, coupling, potential)

    previous = wavefunctions
    current = (hamiltonian(wavefunctions) - CENTER * wavefunctions) / HALF_WIDTH
    for degree_step in range(DEGREE - 1):
        following = 2.0 * (hamiltonian(current) - CENTER * current) / HALF_WIDTH - previous
        previous, current = current, following
    applied = hamiltonian(current)
    projected = jnp.dot(current, applied.T, precision=PRECISE, preferred_element_type=jnp.float32) / NODES
    correlation = jnp.dot(current, current.T, precision=PRECISE, preferred_element_type=jnp.float32) / NODES
    return current, projected, correlation
```

```python
import functools

import jax
import jax.numpy as jnp
from jax import lax
from jax.experimental import pallas as pl
from jax.experimental.pallas import tpu as pltpu
from jax.sharding import PartitionSpec as P

NPROJ = 18
ATOM_DEV = 8
DEGREE = 6
CENTER = 0.9
HALF_WIDTH = 1.1
BANDS = 16
NODES = 1024
NPC = 512
GHOST = 256
LANES = 128
SLOT = 32
F32 = jnp.float32
BF16 = jnp.bfloat16


def dot(a, b):
    return lax.dot_general(a, b, (((1,), (0,)), ((), ())), preferred_element_type=F32)


def dot_nt(a, b):
    return lax.dot_general(a, b, (((1,), (1,)), ((), ())), preferred_element_type=F32)


def split2(x):
    high = x.astype(BF16)
    return high, (x - high.astype(F32)).astype(BF16)


def split3(x):
    high = x.astype(BF16)
    rest = x - high.astype(F32)
    mid = rest.astype(BF16)
    return high, mid, (rest - mid.astype(F32)).astype(BF16)


def product(x_high, x_low, w_high, w_low):
    rows = x_high.shape[0]
    both = dot(jnp.concatenate([x_high, x_low], axis=0), w_high)
    return both[:rows] + both[rows:] + dot(x_high, w_low)


def blocks_of(x):
    return [x[:, i : i + LANES] for i in range(0, x.shape[1], LANES)]


def pick(sources, index, first=0):
    rows = sources[0].shape[0]
    index = jnp.broadcast_to(index, (rows, LANES))
    lane = index & (LANES - 1)
    block = index >> 7
    total = jnp.zeros((rows, LANES), F32)
    for k, source in enumerate(sources):
        value = jnp.take_along_axis(source, lane, axis=1, mode="promise_in_bounds")
        total = jnp.where(block == first + k, value, total)
    return total


def pick_row(sources, index, first=0):
    return jnp.concatenate([pick(sources, i, first) for i in blocks_of(index)], axis=1)


def column(row):
    return jnp.broadcast_to(row, (LANES, row.shape[1])).T


def lane_iota(rows, lanes):
    return lax.broadcasted_iota(jnp.int32, (rows, lanes), 1)


def row_iota(rows, lanes):
    return lax.broadcasted_iota(jnp.int32, (rows, lanes), 0)


def gathered(vectors, conn_ref, send_ref):
    sources = blocks_of(vectors)
    cells = [pick_row(sources, conn_ref[c : c + 1, :]) for c in range(4)]
    return cells, pick_row(sources, send_ref[...])


def padded_projectors(cell):
    return jnp.concatenate([cell, jnp.zeros((SLOT - NPROJ, NPC), F32)], axis=0)


def inner_partials(cells, inner_t_high, inner_t_low):
    x_high, x_low = split2(jnp.concatenate(cells[:3], axis=0))
    wide = product(x_high, x_low, inner_t_high, inner_t_low)
    which = lane_iota(BANDS, LANES) >> 5
    total = jnp.zeros((BANDS, LANES), F32)
    for c in range(3):
        total = jnp.where(which == c, wide[c * BANDS : (c + 1) * BANDS], total)
    return total


def first_kernel(v_ref, conn_ref, send_ref, atom_ref, proj_ref, x_ref, g_ref, up_ref, down_ref, inner_ref):
    cells, ghosts = gathered(v_ref[...], conn_ref, send_ref)
    for c in range(4):
        x_ref[c * BANDS : (c + 1) * BANDS, :] = cells[c]
    g_ref[...] = ghosts
    stacked = jnp.concatenate([padded_projectors(proj_ref[c]) for c in range(3)] + [jnp.zeros((SLOT, NPC), F32)], axis=0)
    inner_high, inner_low = split2(stacked.T)
    inner_ref[0] = inner_high
    inner_ref[1] = inner_low
    partials = inner_partials(cells, inner_high, inner_low)
    which = lane_iota(1, LANES) >> 5
    atoms = jnp.zeros((1, LANES), F32)
    for c in range(4):
        atoms = jnp.where(which == c, atom_ref[c].astype(F32), atoms)
    edge = conn_ref[3:4, :]
    names = column(edge.astype(F32))
    position = row_iota(NPC, LANES).astype(F32)
    inverse = []
    for k in range(GHOST // LANES):
        slot = (lane_iota(NPC, LANES) + (NODES + k * LANES)).astype(F32)
        inverse.append(jnp.max(jnp.where(names == slot, position, -1.0), axis=0, keepdims=True))
    up_ref[...] = jnp.zeros_like(up_ref)
    up_ref[0:BANDS, 0:NPC] = cells[3]
    up_ref[0:BANDS, NPC:] = partials
    up_ref[16 : 16 + NPROJ, 0:NPC] = proj_ref[3]
    up_ref[40:41, 0:NPC] = edge.astype(F32)
    up_ref[41:42, 0:GHOST] = jnp.concatenate(inverse, axis=1)
    up_ref[42:43, 0:LANES] = atoms
    down_ref[...] = jnp.zeros_like(down_ref)
    down_ref[0:BANDS, 0:GHOST] = ghosts
    down_ref[0:BANDS, GHOST:] = partials
    down_ref[16:17, 0:LANES] = atoms


def local_kernel(conn_ref, send_ref, element_ref, e_ref, maps_ref):
    high, low = split2(element_ref[...])
    e_ref[0] = high
    e_ref[1] = low
    least = [jnp.full((1, LANES), 4.0 * NPC, F32)] * (NODES // LANES)
    most = [jnp.full((1, LANES), -1.0, F32)] * (NODES // LANES)
    position = row_iota(NPC, LANES).astype(F32)
    node = lane_iota(NPC, LANES).astype(F32)
    for c in range(4):
        names = column(conn_ref[c : c + 1, :].astype(F32))
        place = position + float(c * NPC)
        for k in range(NODES // LANES):
            same = names == node + float(k * LANES)
            least[k] = jnp.minimum(least[k], jnp.min(jnp.where(same, place, 4.0 * NPC), axis=0, keepdims=True))
            most[k] = jnp.maximum(most[k], jnp.max(jnp.where(same, place, -1.0), axis=0, keepdims=True))
    names = column(send_ref[...].astype(F32))
    maps_ref[...] = jnp.zeros_like(maps_ref)
    for k in range(NODES // LANES):
        here = slice(k * LANES, (k + 1) * LANES)
        maps_ref[0:1, here] = least[k].astype(jnp.int32)
        maps_ref[1:2, here] = jnp.where(most[k] > least[k], most[k], -1.0).astype(jnp.int32)
        same = names == node[:GHOST] + float(k * LANES)
        maps_ref[2:3, here] = jnp.max(jnp.where(same, position[:GHOST], -1.0), axis=0, keepdims=True).astype(jnp.int32)


def joined_kernel(up_ref, down_ref, maps_ref, atom_ref, place_ref, proj_ref, coupling_ref, p_ref, pt_ref, k_ref, coup_ref, index_ref):
    low_atoms, high_atoms = up_ref[42:43, 0:LANES], down_ref[16:17, 0:LANES]
    lane = lane_iota(1, LANES)
    which = lane >> 5
    own = jnp.full((1, LANES), -100.0, F32)
    for c in range(4):
        own = jnp.where(which == c, atom_ref[c].astype(F32), own)
    edge_low = low_atoms[:, 96:97] - float(ATOM_DEV)
    fifth = jnp.where(which == 0, jnp.broadcast_to(edge_low, (1, LANES)), -200.0)
    from_upper = jnp.where(which < 3, high_atoms + float(ATOM_DEV), -300.0)
    from_lower = jnp.where(which < 3, low_atoms - float(ATOM_DEV), -400.0)
    source = jnp.concatenate([own, fifth, from_upper, from_lower], axis=1)
    inside = (lane_iota(SLOT, 4 * LANES) & (SLOT - 1)) == row_iota(SLOT, 4 * LANES)
    rows = []
    for c in range(8):
        if c < 4:
            same = source == atom_ref[c].astype(F32)
        elif c == 4:
            same = source == jnp.broadcast_to(edge_low, source.shape)
        else:
            same = source == 1000.0
        rows.append(jnp.where(inside & jnp.broadcast_to(same, inside.shape), 1.0, 0.0))
    k_ref[...] = jnp.concatenate(rows, axis=0).T.astype(BF16)
    lower = coupling_ref[pl.ds(pl.multiple_of(place_ref[0] * ATOM_DEV, ATOM_DEV), ATOM_DEV), :]
    mine = coupling_ref[pl.ds(pl.multiple_of(place_ref[1] * ATOM_DEV, ATOM_DEV), ATOM_DEV), :]
    pair = jnp.concatenate([lower, mine], axis=0)
    pair = jnp.concatenate([pair, jnp.zeros((2 * ATOM_DEV, SLOT - NPROJ), F32)], axis=1)
    wide = jnp.concatenate([pair] * 8, axis=1)
    target = source[:, : 2 * LANES]
    slot = row_iota(2 * ATOM_DEV, 2 * LANES).astype(F32)
    chosen = jnp.where(jnp.broadcast_to(target, slot.shape) == slot, wide, 0.0)
    coup_ref[...] = jnp.broadcast_to(jnp.sum(chosen, axis=0, keepdims=True), coup_ref.shape)
    parts = [padded_projectors(proj_ref[c]) for c in range(4)]
    parts.append(padded_projectors(up_ref[16 : 16 + NPROJ, 0:NPC]))
    parts.append(jnp.zeros((3 * SLOT, NPC), F32))
    stacked = jnp.concatenate(parts, axis=0)
    p_ref[0], p_ref[1] = split2(stacked)
    pt_ref[0], pt_ref[1] = split2(stacked.T)
    inverse = up_ref[41:42, 0:GHOST]
    index_ref[...] = jnp.zeros_like(index_ref)
    index_ref[0:2, :] = maps_ref[0:2, :]
    sent = maps_ref[2:3, :]
    rows8 = [jnp.broadcast_to(b, (8, LANES)) for b in blocks_of(inverse)]
    third = pick_row(rows8, sent)
    third = jnp.where(jnp.broadcast_to(sent, third.shape) >= 0, third, -1.0)
    index_ref[2:3, :] = third[0:1].astype(jnp.int32)
    index_ref[3:4, 0:NPC] = up_ref[40:41, 0:NPC].astype(jnp.int32) - NODES


def apply(v, x_ref, g_ref, up_ref, down_ref, conn_ref, index_ref, pot_ref, e_ref, p_ref, pt_ref, k_ref, coup_ref):
    edge = x_ref[48:64, :] + pick_row(blocks_of(down_ref[0:BANDS, 0:GHOST]), conn_ref[3:4, :] - NODES)
    low = up_ref[0:BANDS, 0:NPC] + pick_row(blocks_of(g_ref[...]), index_ref[3:4, 0:NPC])
    x_high, x_low = split2(jnp.concatenate([x_ref[0:48, :], edge, low], axis=0))
    wide = product(x_high, x_low, pt_ref[0], pt_ref[1])
    which = lane_iota(BANDS, 2 * LANES) >> 5
    own = jnp.zeros((BANDS, 2 * LANES), F32)
    for c in range(5):
        own = jnp.where(which == c, wide[c * BANDS : (c + 1) * BANDS], own)
    partials = jnp.concatenate([own, down_ref[0:BANDS, GHOST:], up_ref[0:BANDS, NPC:]], axis=1)
    sums = dot(jnp.concatenate(split3(partials), axis=0), k_ref[...])
    weights = (sums[0:16] + sums[16:32] + sums[32:48]) * coup_ref[0:1, :]
    spread = jnp.concatenate([jnp.where(which == c, weights, 0.0) for c in range(5)], axis=0)
    c_high, c_low = split2(spread)
    y = product(x_high, x_low, e_ref[0], e_ref[1]) + product(c_high, c_low, p_ref[0], p_ref[1])
    cells = []
    for c in range(5):
        cells += blocks_of(y[c * BANDS : (c + 1) * BANDS])
    out = []
    for k in range(NODES // LANES):
        here = slice(k * LANES, (k + 1) * LANES)
        total = pick(cells[:16], index_ref[0:1, here]) + pick(cells[:16], index_ref[1:2, here])
        out.append(total + pick(cells[16:], index_ref[2:3, here]))
    return jnp.concatenate(out, axis=1) + pot_ref[...] * v


def step_kernel(first, v_ref, prev_ref, x_ref, g_ref, up_ref, down_ref, conn_ref, send_ref, index_ref, pot_ref, e_ref, p_ref, pt_ref,
                k_ref, coup_ref, inner_ref, new_ref, xo_ref, go_ref, upo_ref, downo_ref):
    v = v_ref[...]
    h = apply(v, x_ref, g_ref, up_ref, down_ref, conn_ref, index_ref, pot_ref, e_ref, p_ref, pt_ref, k_ref, coup_ref)
    if first:
        new = (h - CENTER * v) * (1.0 / HALF_WIDTH)
    else:
        new = (h - CENTER * v) * (2.0 / HALF_WIDTH) - prev_ref[...]
    new_ref[...] = new
    cells, ghosts = gathered(new, conn_ref, send_ref)
    for c in range(4):
        xo_ref[c * BANDS : (c + 1) * BANDS, :] = cells[c]
    go_ref[...] = ghosts
    partials = inner_partials(cells, inner_ref[0], inner_ref[1])
    upo_ref[:, 0:NPC] = cells[3]
    upo_ref[:, NPC:] = partials
    downo_ref[:, 0:GHOST] = ghosts
    downo_ref[:, GHOST:] = partials


def gram_kernel(v_ref, all_ref, x_ref, g_ref, up_ref, down_ref, conn_ref, index_ref, pot_ref, e_ref, p_ref, pt_ref, k_ref, coup_ref,
                out_ref):
    v = v_ref[...]
    h = apply(v, x_ref, g_ref, up_ref, down_ref, conn_ref, index_ref, pot_ref, e_ref, p_ref, pt_ref, k_ref, coup_ref)
    s_high, s_low = split2(jnp.concatenate([h, v], axis=0))
    a_high, a_low = split2(all_ref[...])
    both = dot_nt(jnp.concatenate([s_high, s_low], axis=0), a_high)
    panel = both[:32] + both[32:] + dot_nt(s_high, a_low)
    for i in range(out_ref.shape[0]):
        out_ref[i] = panel


def add_kernel(parts_ref, out_ref):
    total = parts_ref[0]
    for i in range(1, parts_ref.shape[0]):
        total = total + parts_ref[i]
    for i in range(out_ref.shape[0]):
        out_ref[i] = total


def last_kernel(scale, parts_ref, projected_ref, correlation_ref):
    total = parts_ref[0]
    for i in range(1, parts_ref.shape[0]):
        total = total + parts_ref[i]
    flipped = (total * scale).T
    projected_ref[...] = flipped[:, 0:BANDS]
    correlation_ref[...] = flipped[:, BANDS:]


VM = pl.BlockSpec(memory_space=pltpu.VMEM)
SM = pl.BlockSpec(memory_space=pltpu.SMEM)


def call(kernel, outs, ins, *args):
    return pl.pallas_call(
        kernel,
        out_shape=[jax.ShapeDtypeStruct(s, t) for s, t in outs],
        in_specs=ins,
        out_specs=[VM] * len(outs),
        compiler_params=pltpu.CompilerParams(vmem_limit_bytes=40 * 2**20),
    )(*args)


def shifted(block, distance):
    size = lax.axis_size("fe")
    return lax.ppermute(block, "fe", [(i, (i + distance) % size) for i in range(size)])


def on_device(wavefunctions, potential, element_matrix, projectors, coupling, connectivity, send_list, atom_of_cell):
    fe_count = lax.axis_size("fe")
    fe = lax.axis_index("fe").astype(jnp.int32)
    place = jnp.stack([(fe + fe_count - 1) % fe_count, fe])
    send = send_list.reshape(1, GHOST)
    pot = potential.reshape(1, NODES)
    x, g, up, down, inner = call(
        first_kernel,
        [((64, NPC), F32), ((BANDS, GHOST), F32), ((48, 640), F32), ((24, 384), F32), ((2, NPC, LANES), BF16)],
        [VM, VM, VM, SM, VM],
        wavefunctions, connectivity, send, atom_of_cell, projectors,
    )
    up, down = shifted(up, 1), shifted(down, -1)
    e, maps = call(
        local_kernel,
        [((2, NPC, NPC), BF16), ((8, NODES), jnp.int32)],
        [VM, VM, VM],
        connectivity, send, element_matrix,
    )
    p, pt, k, coup, index = call(
        joined_kernel,
        [((2, 256, NPC), BF16), ((2, NPC, 256), BF16), ((512, 256), BF16), ((8, 256), F32), ((8, NODES), jnp.int32)],
        [VM, VM, VM, SM, SM, VM, VM],
        up, down, maps, atom_of_cell, place, projectors, coupling,
    )
    previous = current = wavefunctions
    for step in range(DEGREE):
        new, x, g, up, down = call(
            functools.partial(step_kernel, step == 0),
            [((BANDS, NODES), F32), ((64, NPC), F32), ((BANDS, GHOST), F32), ((BANDS, 640), F32), ((BANDS, 384), F32)],
            [VM] * 16,
            current, previous, x, g, up, down, connectivity, send, index, pot, e, p, pt, k, coup, inner,
        )
        previous, current = current, new
        up, down = shifted(up, 1), shifted(down, -1)
    everyone = lax.all_gather(current, "band", axis=0, tiled=True)
    (copies,) = call(
        gram_kernel,
        [((4, 32, LANES), F32)],
        [VM] * 14,
        current, everyone, x, g, up, down, connectivity, index, pot, e, p, pt, k, coup,
    )
    near = [[4 * i + j for j in range(4)] for i in range(fe_count // 4)]
    far = [[4 * i + j for i in range(fe_count // 4)] for j in range(4)]
    parts = lax.all_to_all(copies, "fe", 0, 0, axis_index_groups=near)
    (copies,) = call(add_kernel, [((fe_count // 4, 32, LANES), F32)], [VM], parts)
    parts = lax.all_to_all(copies, "fe", 0, 0, axis_index_groups=far)
    projected, correlation = call(
        functools.partial(last_kernel, 1.0 / (NODES * fe_count)),
        [((LANES, BANDS), F32), ((LANES, BANDS), F32)],
        [VM],
        parts,
    )
    return current, projected, correlation


def solution(mesh):
    in_specs = (
        P("band", "fe"),
        P("fe"),
        P(),
        P("fe", None, None),
        P(),
        P("fe", None),
        P("fe"),
        P("fe"),
    )
    out_specs = (P("band", "fe"), P(None, "band"), P(None, "band"))
    return jax.shard_map(on_device, mesh=mesh, in_specs=in_specs, out_specs=out_specs, check_vma=False)
```

```python
import functools

import jax
import jax.numpy as jnp
from jax import lax
from jax.experimental import pallas as pl
from jax.experimental.pallas import tpu as pltpu
from jax.sharding import PartitionSpec as P

NPROJ = 18
ATOM_DEV = 8
DEGREE = 6
CENTER = 0.9
HALF_WIDTH = 1.1
BANDS = 16
NODES = 1024
NPC = 512
GHOST = 256
LANES = 128
SLOT = 32
F32 = jnp.float32
BF16 = jnp.bfloat16


def dot(a, b):
    return lax.dot_general(a, b, (((1,), (0,)), ((), ())), preferred_element_type=F32)


def dot_nt(a, b):
    return lax.dot_general(a, b, (((1,), (1,)), ((), ())), preferred_element_type=F32)


def split2(x):
    high = x.astype(BF16)
    return high, (x - high.astype(F32)).astype(BF16)


def split3(x):
    high = x.astype(BF16)
    rest = x - high.astype(F32)
    mid = rest.astype(BF16)
    return high, mid, (rest - mid.astype(F32)).astype(BF16)


def product(x_high, x_low, w_high, w_low):
    rows = x_high.shape[0]
    both = dot(jnp.concatenate([x_high, x_low], axis=0), w_high)
    return both[:rows] + both[rows:] + dot(x_high, w_low)


def blocks_of(x):
    return [x[:, i : i + LANES] for i in range(0, x.shape[1], LANES)]


def pick(sources, index, first=0):
    rows = sources[0].shape[0]
    index = jnp.broadcast_to(index, (rows, LANES))
    lane = index & (LANES - 1)
    block = index >> 7
    total = jnp.zeros((rows, LANES), F32)
    for k, source in enumerate(sources):
        value = jnp.take_along_axis(source, lane, axis=1, mode="promise_in_bounds")
        total = jnp.where(block == first + k, value, total)
    return total


def pick_row(sources, index, first=0):
    return jnp.concatenate([pick(sources, i, first) for i in blocks_of(index)], axis=1)


def column(row):
    return jnp.broadcast_to(row, (LANES, row.shape[1])).T


def lane_iota(rows, lanes):
    return lax.broadcasted_iota(jnp.int32, (rows, lanes), 1)


def row_iota(rows, lanes):
    return lax.broadcasted_iota(jnp.int32, (rows, lanes), 0)


def gathered(vectors, conn_ref, send_ref):
    sources = blocks_of(vectors)
    cells = [pick_row(sources, conn_ref[c : c + 1, :]) for c in range(4)]
    return cells, pick_row(sources, send_ref[...])


def padded_projectors(cell):
    return jnp.concatenate([cell, jnp.zeros((SLOT - NPROJ, NPC), F32)], axis=0)


def inner_partials(cells, inner_t_high, inner_t_low):
    x_high, x_low = split2(jnp.concatenate(cells[:3], axis=0))
    wide = product(x_high, x_low, inner_t_high, inner_t_low)
    which = lane_iota(BANDS, LANES) >> 5
    total = jnp.zeros((BANDS, LANES), F32)
    for c in range(3):
        total = jnp.where(which == c, wide[c * BANDS : (c + 1) * BANDS], total)
    return total


def first_kernel(v_ref, conn_ref, send_ref, atom_ref, proj_ref, x_ref, g_ref, up_ref, down_ref, inner_ref):
    cells, ghosts = gathered(v_ref[...], conn_ref, send_ref)
    for c in range(4):
        x_ref[c * BANDS : (c + 1) * BANDS, :] = cells[c]
    g_ref[...] = ghosts
    stacked = jnp.concatenate([padded_projectors(proj_ref[c]) for c in range(3)] + [jnp.zeros((SLOT, NPC), F32)], axis=0)
    inner_high, inner_low = split2(stacked.T)
    inner_ref[0] = inner_high
    inner_ref[1] = inner_low
    partials = inner_partials(cells, inner_high, inner_low)
    which = lane_iota(1, LANES) >> 5
    atoms = jnp.zeros((1, LANES), F32)
    for c in range(4):
        atoms = jnp.where(which == c, atom_ref[c].astype(F32), atoms)
    edge = conn_ref[3:4, :]
    names = column(edge.astype(F32))
    position = row_iota(NPC, LANES).astype(F32)
    inverse = []
    for k in range(GHOST // LANES):
        slot = (lane_iota(NPC, LANES) + (NODES + k * LANES)).astype(F32)
        inverse.append(jnp.max(jnp.where(names == slot, position, -1.0), axis=0, keepdims=True))
    up_ref[...] = jnp.zeros_like(up_ref)
    up_ref[0:BANDS, 0:NPC] = cells[3]
    up_ref[0:BANDS, NPC:] = partials
    up_ref[16 : 16 + NPROJ, 0:NPC] = proj_ref[3]
    up_ref[40:41, 0:NPC] = edge.astype(F32)
    up_ref[41:42, 0:GHOST] = jnp.concatenate(inverse, axis=1)
    up_ref[42:43, 0:LANES] = atoms
    down_ref[...] = jnp.zeros_like(down_ref)
    down_ref[0:BANDS, 0:GHOST] = ghosts
    down_ref[0:BANDS, GHOST:] = partials
    down_ref[16:17, 0:LANES] = atoms


def local_kernel(conn_ref, send_ref, element_ref, e_ref, maps_ref):
    high, low = split2(element_ref[...])
    e_ref[0] = high
    e_ref[1] = low
    least = [jnp.full((1, LANES), 4.0 * NPC, F32)] * (NODES // LANES)
    most = [jnp.full((1, LANES), -1.0, F32)] * (NODES // LANES)
    position = row_iota(NPC, LANES).astype(F32)
    node = lane_iota(NPC, LANES).astype(F32)
    for c in range(4):
        names = column(conn_ref[c : c + 1, :].astype(F32))
        place = position + float(c * NPC)
        for k in range(NODES // LANES):
            same = names == node + float(k * LANES)
            least[k] = jnp.minimum(least[k], jnp.min(jnp.where(same, place, 4.0 * NPC), axis=0, keepdims=True))
            most[k] = jnp.maximum(most[k], jnp.max(jnp.where(same, place, -1.0), axis=0, keepdims=True))
    names = column(send_ref[...].astype(F32))
    maps_ref[...] = jnp.zeros_like(maps_ref)
    for k in range(NODES // LANES):
        here = slice(k * LANES, (k + 1) * LANES)
        maps_ref[0:1, here] = least[k].astype(jnp.int32)
        maps_ref[1:2, here] = jnp.where(most[k] > least[k], most[k], -1.0).astype(jnp.int32)
        same = names == node[:GHOST] + float(k * LANES)
        maps_ref[2:3, here] = jnp.max(jnp.where(same, position[:GHOST], -1.0), axis=0, keepdims=True).astype(jnp.int32)


def joined_kernel(up_ref, down_ref, maps_ref, atom_ref, place_ref, proj_ref, coupling_ref, p_ref, pt_ref, k_ref, coup_ref, index_ref):
    low_atoms, high_atoms = up_ref[42:43, 0:LANES], down_ref[16:17, 0:LANES]
    lane = lane_iota(1, LANES)
    which = lane >> 5
    own = jnp.full((1, LANES), -100.0, F32)
    for c in range(4):
        own = jnp.where(which == c, atom_ref[c].astype(F32), own)
    edge_low = low_atoms[:, 96:97] - float(ATOM_DEV)
    fifth = jnp.where(which == 0, jnp.broadcast_to(edge_low, (1, LANES)), -200.0)
    from_upper = jnp.where(which < 3, high_atoms + float(ATOM_DEV), -300.0)
    from_lower = jnp.where(which < 3, low_atoms - float(ATOM_DEV), -400.0)
    source = jnp.concatenate([own, fifth, from_upper, from_lower], axis=1)
    inside = (lane_iota(SLOT, 4 * LANES) & (SLOT - 1)) == row_iota(SLOT, 4 * LANES)
    rows = []
    for c in range(8):
        if c < 4:
            same = source == atom_ref[c].astype(F32)
        elif c == 4:
            same = source == jnp.broadcast_to(edge_low, source.shape)
        else:
            same = source == 1000.0
        rows.append(jnp.where(inside & jnp.broadcast_to(same, inside.shape), 1.0, 0.0))
    k_ref[...] = jnp.concatenate(rows, axis=0).T.astype(BF16)
    lower = coupling_ref[pl.ds(pl.multiple_of(place_ref[0] * ATOM_DEV, ATOM_DEV), ATOM_DEV), :]
    mine = coupling_ref[pl.ds(pl.multiple_of(place_ref[1] * ATOM_DEV, ATOM_DEV), ATOM_DEV), :]
    pair = jnp.concatenate([lower, mine], axis=0)
    pair = jnp.concatenate([pair, jnp.zeros((2 * ATOM_DEV, SLOT - NPROJ), F32)], axis=1)
    wide = jnp.concatenate([pair] * 8, axis=1)
    target = source[:, : 2 * LANES]
    slot = row_iota(2 * ATOM_DEV, 2 * LANES).astype(F32)
    chosen = jnp.where(jnp.broadcast_to(target, slot.shape) == slot, wide, 0.0)
    coup_ref[...] = jnp.broadcast_to(jnp.sum(chosen, axis=0, keepdims=True), coup_ref.shape)
    parts = [padded_projectors(proj_ref[c]) for c in range(4)]
    parts.append(padded_projectors(up_ref[16 : 16 + NPROJ, 0:NPC]))
    parts.append(jnp.zeros((3 * SLOT, NPC), F32))
    stacked = jnp.concatenate(parts, axis=0)
    p_ref[0], p_ref[1] = split2(stacked)
    pt_ref[0], pt_ref[1] = split2(stacked.T)
    inverse = up_ref[41:42, 0:GHOST]
    index_ref[...] = jnp.zeros_like(index_ref)
    index_ref[0:2, :] = maps_ref[0:2, :]
    sent = maps_ref[2:3, :]
    rows8 = [jnp.broadcast_to(b, (8, LANES)) for b in blocks_of(inverse)]
    third = pick_row(rows8, sent)
    third = jnp.where(jnp.broadcast_to(sent, third.shape) >= 0, third, -1.0)
    index_ref[2:3, :] = third[0:1].astype(jnp.int32)
    index_ref[3:4, 0:NPC] = up_ref[40:41, 0:NPC].astype(jnp.int32) - NODES


def apply(v, x_ref, g_ref, up_ref, down_ref, conn_ref, index_ref, pot_ref, e_ref, p_ref, pt_ref, k_ref, coup_ref):
    edge = x_ref[48:64, :] + pick_row(blocks_of(down_ref[0:BANDS, 0:GHOST]), conn_ref[3:4, :] - NODES)
    low = up_ref[0:BANDS, 0:NPC] + pick_row(blocks_of(g_ref[...]), index_ref[3:4, 0:NPC])
    x_high, x_low = split2(jnp.concatenate([x_ref[0:48, :], edge, low], axis=0))
    wide = product(x_high, x_low, pt_ref[0], pt_ref[1])
    which = lane_iota(BANDS, 2 * LANES) >> 5
    own = jnp.zeros((BANDS, 2 * LANES), F32)
    for c in range(5):
        own = jnp.where(which == c, wide[c * BANDS : (c + 1) * BANDS], own)
    partials = jnp.concatenate([own, down_ref[0:BANDS, GHOST:], up_ref[0:BANDS, NPC:]], axis=1)
    sums = dot(jnp.concatenate(split3(partials), axis=0), k_ref[...])
    weights = (sums[0:16] + sums[16:32] + sums[32:48]) * coup_ref[0:1, :]
    spread = jnp.concatenate([jnp.where(which == c, weights, 0.0) for c in range(5)], axis=0)
    c_high, c_low = split2(spread)
    y = product(x_high, x_low, e_ref[0], e_ref[1]) + product(c_high, c_low, p_ref[0], p_ref[1])
    cells = []
    for c in range(5):
        cells += blocks_of(y[c * BANDS : (c + 1) * BANDS])
    out = []
    for k in range(NODES // LANES):
        here = slice(k * LANES, (k + 1) * LANES)
        total = pick(cells[:16], index_ref[0:1, here]) + pick(cells[:16], index_ref[1:2, here])
        out.append(total + pick(cells[16:], index_ref[2:3, here]))
    return jnp.concatenate(out, axis=1) + pot_ref[...] * v


def step_kernel(first, v_ref, prev_ref, x_ref, g_ref, up_ref, down_ref, conn_ref, send_ref, index_ref, pot_ref, e_ref, p_ref, pt_ref,
                k_ref, coup_ref, inner_ref, new_ref, xo_ref, go_ref, upo_ref, downo_ref):
    v = v_ref[...]
    h = apply(v, x_ref, g_ref, up_ref, down_ref, conn_ref, index_ref, pot_ref, e_ref, p_ref, pt_ref, k_ref, coup_ref)
    if first:
        new = (h - CENTER * v) * (1.0 / HALF_WIDTH)
    else:
        new = (h - CENTER * v) * (2.0 / HALF_WIDTH) - prev_ref[...]
    new_ref[...] = new
    cells, ghosts = gathered(new, conn_ref, send_ref)
    for c in range(4):
        xo_ref[c * BANDS : (c + 1) * BANDS, :] = cells[c]
    go_ref[...] = ghosts
    partials = inner_partials(cells, inner_ref[0], inner_ref[1])
    upo_ref[:, 0:NPC] = cells[3]
    upo_ref[:, NPC:] = partials
    downo_ref[:, 0:GHOST] = ghosts
    downo_ref[:, GHOST:] = partials


def gram_kernel(v_ref, all_ref, x_ref, g_ref, up_ref, down_ref, conn_ref, index_ref, pot_ref, e_ref, p_ref, pt_ref, k_ref, coup_ref,
                out_ref):
    v = v_ref[...]
    h = apply(v, x_ref, g_ref, up_ref, down_ref, conn_ref, index_ref, pot_ref, e_ref, p_ref, pt_ref, k_ref, coup_ref)
    s_high, s_low = split2(jnp.concatenate([h, v], axis=0))
    a_high, a_low = split2(all_ref[...])
    both = dot_nt(jnp.concatenate([s_high, s_low], axis=0), a_high)
    panel = both[:32] + both[32:] + dot_nt(s_high, a_low)
    for i in range(out_ref.shape[0]):
        out_ref[i] = panel


def add_kernel(parts_ref, out_ref):
    total = parts_ref[0]
    for i in range(1, parts_ref.shape[0]):
        total = total + parts_ref[i]
    for i in range(out_ref.shape[0]):
        out_ref[i] = total


def last_kernel(scale, parts_ref, projected_ref, correlation_ref):
    total = parts_ref[0]
    for i in range(1, parts_ref.shape[0]):
        total = total + parts_ref[i]
    projected_ref[...] = total[0:BANDS] * scale
    correlation_ref[...] = total[BANDS:] * scale


VM = pl.BlockSpec(memory_space=pltpu.VMEM)
SM = pl.BlockSpec(memory_space=pltpu.SMEM)


def call(kernel, outs, ins, *args):
    return pl.pallas_call(
        kernel,
        out_shape=[jax.ShapeDtypeStruct(s, t) for s, t in outs],
        in_specs=ins,
        out_specs=[VM] * len(outs),
        compiler_params=pltpu.CompilerParams(vmem_limit_bytes=40 * 2**20),
    )(*args)


def shifted(block, distance):
    size = lax.axis_size("fe")
    return lax.ppermute(block, "fe", [(i, (i + distance) % size) for i in range(size)])


def on_device(wavefunctions, potential, element_matrix, projectors, coupling, connectivity, send_list, atom_of_cell):
    fe_count = lax.axis_size("fe")
    fe = lax.axis_index("fe").astype(jnp.int32)
    place = jnp.stack([(fe + fe_count - 1) % fe_count, fe])
    send = send_list.reshape(1, GHOST)
    pot = potential.reshape(1, NODES)
    x, g, up, down, inner = call(
        first_kernel,
        [((64, NPC), F32), ((BANDS, GHOST), F32), ((48, 640), F32), ((24, 384), F32), ((2, NPC, LANES), BF16)],
        [VM, VM, VM, SM, VM],
        wavefunctions, connectivity, send, atom_of_cell, projectors,
    )
    up, down = shifted(up, 1), shifted(down, -1)
    e, maps = call(
        local_kernel,
        [((2, NPC, NPC), BF16), ((8, NODES), jnp.int32)],
        [VM, VM, VM],
        connectivity, send, element_matrix,
    )
    p, pt, k, coup, index = call(
        joined_kernel,
        [((2, 256, NPC), BF16), ((2, NPC, 256), BF16), ((512, 256), BF16), ((8, 256), F32), ((8, NODES), jnp.int32)],
        [VM, VM, VM, SM, SM, VM, VM],
        up, down, maps, atom_of_cell, place, projectors, coupling,
    )
    previous = current = wavefunctions
    for step in range(DEGREE):
        new, x, g, up, down = call(
            functools.partial(step_kernel, step == 0),
            [((BANDS, NODES), F32), ((64, NPC), F32), ((BANDS, GHOST), F32), ((BANDS, 640), F32), ((BANDS, 384), F32)],
            [VM] * 16,
            current, previous, x, g, up, down, connectivity, send, index, pot, e, p, pt, k, coup, inner,
        )
        previous, current = current, new
        if step == DEGREE - 1:
            bands = lax.axis_size("band")
            everyone = lax.all_to_all(jnp.broadcast_to(current[None], (bands,) + current.shape), "band", 0, 0)
            everyone = everyone.reshape(bands * BANDS, NODES)
        up, down = shifted(up, 1), shifted(down, -1)
    (copies,) = call(
        gram_kernel,
        [((4, 32, LANES), F32)],
        [VM] * 14,
        current, everyone, x, g, up, down, connectivity, index, pot, e, p, pt, k, coup,
    )
    near = [[4 * i + j for j in range(4)] for i in range(fe_count // 4)]
    far = [[4 * i + j for i in range(fe_count // 4)] for j in range(4)]
    parts = lax.all_to_all(copies, "fe", 0, 0, axis_index_groups=near)
    (copies,) = call(add_kernel, [((fe_count // 4, 32, LANES), F32)], [VM], parts)
    parts = lax.all_to_all(copies, "fe", 0, 0, axis_index_groups=far)
    projected, correlation = call(
        functools.partial(last_kernel, 1.0 / (NODES * fe_count)),
        [((BANDS, LANES), F32), ((BANDS, LANES), F32)],
        [VM],
        parts,
    )
    return current, projected.T, correlation.T


def solution(mesh):
    in_specs = (
        P("band", "fe"),
        P("fe"),
        P(),
        P("fe", None, None),
        P(),
        P("fe", None),
        P("fe"),
        P("fe"),
    )
    out_specs = (P("band", "fe"), P(None, "band"), P(None, "band"))
    return jax.shard_map(on_device, mesh=mesh, in_specs=in_specs, out_specs=out_specs, check_vma=False)
```

```python
import functools

import jax
import jax.numpy as jnp
from jax import lax
from jax.experimental import pallas as pl
from jax.experimental.pallas import tpu as pltpu
from jax.sharding import PartitionSpec as P

NPROJ = 18
ATOM_DEV = 8
DEGREE = 6
CENTER = 0.9
HALF_WIDTH = 1.1
BANDS = 16
NODES = 1024
NPC = 512
GHOST = 256
LANES = 128
SLOT = 32
F32 = jnp.float32
BF16 = jnp.bfloat16


def dot(a, b):
    return lax.dot_general(a, b, (((1,), (0,)), ((), ())), preferred_element_type=F32)


def dot_nt(a, b):
    return lax.dot_general(a, b, (((1,), (1,)), ((), ())), preferred_element_type=F32)


def split2(x):
    high = x.astype(BF16)
    return high, (x - high.astype(F32)).astype(BF16)


def split3(x):
    high = x.astype(BF16)
    rest = x - high.astype(F32)
    mid = rest.astype(BF16)
    return high, mid, (rest - mid.astype(F32)).astype(BF16)


def product(x_high, x_low, w_high, w_low):
    rows = x_high.shape[0]
    both = dot(jnp.concatenate([x_high, x_low], axis=0), w_high)
    return both[:rows] + both[rows:] + dot(x_high, w_low)


def blocks_of(x):
    return [x[:, i : i + LANES] for i in range(0, x.shape[1], LANES)]


def pick(sources, index, first=0):
    rows = sources[0].shape[0]
    index = jnp.broadcast_to(index, (rows, LANES))
    lane = index & (LANES - 1)
    block = index >> 7
    total = jnp.zeros((rows, LANES), F32)
    for k, source in enumerate(sources):
        value = jnp.take_along_axis(source, lane, axis=1, mode="promise_in_bounds")
        total = jnp.where(block == first + k, value, total)
    return total


def pick_row(sources, index, first=0):
    return jnp.concatenate([pick(sources, i, first) for i in blocks_of(index)], axis=1)


def column(row):
    return jnp.broadcast_to(row, (LANES, row.shape[1])).T


def lane_iota(rows, lanes):
    return lax.broadcasted_iota(jnp.int32, (rows, lanes), 1)


def row_iota(rows, lanes):
    return lax.broadcasted_iota(jnp.int32, (rows, lanes), 0)


def padded_projectors(cell):
    return jnp.concatenate([cell, jnp.zeros((SLOT - NPROJ, NPC), F32)], axis=0)


def pack_message(vectors, partials, conn_ref, send_ref, up_ref, down_ref):
    sources = blocks_of(vectors)
    up_ref[0:BANDS, 0:NPC] = pick_row(sources, conn_ref[3:4, :])
    up_ref[0:BANDS, NPC:] = partials
    down_ref[0:BANDS, 0:GHOST] = pick_row(sources, send_ref[...])
    down_ref[0:BANDS, GHOST:] = partials


def first_kernel(v_ref, conn_ref, send_ref, atom_ref, proj_ref, up_ref, down_ref):
    v = v_ref[...]
    sources = blocks_of(v)
    cells = [pick_row(sources, conn_ref[c : c + 1, :]) for c in range(3)]
    stacked = [padded_projectors(proj_ref[:, c, :]) for c in range(3)] + [jnp.zeros((SLOT, NPC), F32)]
    t_high, t_low = split2(jnp.concatenate(stacked, axis=0).T)
    x_high, x_low = split2(jnp.concatenate(cells, axis=0))
    wide = product(x_high, x_low, t_high, t_low)
    which = lane_iota(BANDS, LANES) >> 5
    partials = jnp.zeros((BANDS, LANES), F32)
    for c in range(3):
        partials = jnp.where(which == c, wide[c * BANDS : (c + 1) * BANDS], partials)
    which = lane_iota(1, LANES) >> 5
    atoms = jnp.zeros((1, LANES), F32)
    for c in range(4):
        atoms = jnp.where(which == c, atom_ref[c].astype(F32), atoms)
    edge = conn_ref[3:4, :]
    names = column(edge.astype(F32))
    position = row_iota(NPC, LANES).astype(F32)
    inverse = []
    for k in range(GHOST // LANES):
        slot = (lane_iota(NPC, LANES) + (NODES + k * LANES)).astype(F32)
        inverse.append(jnp.max(jnp.where(names == slot, position, -1.0), axis=0, keepdims=True))
    up_ref[...] = jnp.zeros_like(up_ref)
    down_ref[...] = jnp.zeros_like(down_ref)
    pack_message(v, partials, conn_ref, send_ref, up_ref, down_ref)
    up_ref[16 : 16 + NPROJ, 0:NPC] = proj_ref[:, 3, :]
    up_ref[40:41, 0:NPC] = edge.astype(F32)
    up_ref[41:42, 0:GHOST] = jnp.concatenate(inverse, axis=1)
    up_ref[42:43, 0:LANES] = atoms
    down_ref[16:17, 0:LANES] = atoms


def local_kernel(conn_ref, send_ref, element_ref, proj_ref, down_ref, e_ref, maps_ref, p_ref, pt_ref, downo_ref):
    downo_ref[...] = down_ref[...]
    high, low = split2(element_ref[...])
    e_ref[0] = high
    e_ref[1] = low
    least = [jnp.full((1, LANES), 4.0 * NPC, F32)] * (NODES // LANES)
    most = [jnp.full((1, LANES), -1.0, F32)] * (NODES // LANES)
    position = row_iota(NPC, LANES).astype(F32)
    node = lane_iota(NPC, LANES).astype(F32)
    for c in range(4):
        names = column(conn_ref[c : c + 1, :].astype(F32))
        place = position + float(c * NPC)
        thirds = jnp.concatenate(split3(padded_projectors(proj_ref[:, c, :])), axis=0)
        for k in range(0, NODES // LANES, 2):
            hits = []
            for j in (k, k + 1):
                same = names == node + float(j * LANES)
                least[j] = jnp.minimum(least[j], jnp.min(jnp.where(same, place, 4.0 * NPC), axis=0, keepdims=True))
                most[j] = jnp.maximum(most[j], jnp.max(jnp.where(same, place, -1.0), axis=0, keepdims=True))
                hits.append(jnp.where(same, 1.0, 0.0).astype(BF16))
            parts = dot(thirds, jnp.concatenate(hits, axis=1))
            p_ref[c * SLOT : (c + 1) * SLOT, k * LANES : (k + 2) * LANES] = parts[:SLOT] + parts[SLOT : 2 * SLOT] + parts[2 * SLOT :]
    inner = jnp.concatenate([p_ref[0 : 3 * SLOT, :], jnp.zeros((SLOT, NODES), F32)], axis=0)
    pt_ref[0], pt_ref[1] = split2(inner.T)
    names = column(send_ref[...].astype(F32))
    maps_ref[...] = jnp.zeros_like(maps_ref)
    for k in range(NODES // LANES):
        here = slice(k * LANES, (k + 1) * LANES)
        maps_ref[0:1, here] = least[k].astype(jnp.int32)
        maps_ref[1:2, here] = jnp.where(most[k] > least[k], most[k], -1.0).astype(jnp.int32)
        same = names == node[:GHOST] + float(k * LANES)
        maps_ref[2:3, here] = jnp.max(jnp.where(same, position[:GHOST], -1.0), axis=0, keepdims=True).astype(jnp.int32)


def joined_kernel(up_ref, down_ref, maps_ref, atom_ref, place_ref, proj_ref, coupling_ref, pn_ref, p_ref, pe_ref, k_ref, coup_ref, index_ref):
    low_atoms, high_atoms = up_ref[42:43, 0:LANES], down_ref[16:17, 0:LANES]
    which = lane_iota(1, LANES) >> 5
    own = jnp.full((1, LANES), -100.0, F32)
    for c in range(4):
        own = jnp.where(which == c, atom_ref[c].astype(F32), own)
    edge_low = jnp.broadcast_to(low_atoms[:, 96:97] - float(ATOM_DEV), (1, LANES))
    edges = jnp.where(which == 0, atom_ref[3].astype(F32), jnp.where(which == 1, edge_low, -200.0))
    from_upper = jnp.where(which < 3, high_atoms + float(ATOM_DEV), -300.0)
    from_lower = jnp.where(which < 3, low_atoms - float(ATOM_DEV), -400.0)
    source = jnp.concatenate([jnp.where(which < 3, own, -500.0), edges, from_upper, from_lower], axis=1)
    inside = (lane_iota(SLOT, 4 * LANES) & (SLOT - 1)) == row_iota(SLOT, 4 * LANES)
    rows = []
    for c in range(5):
        if c < 4:
            same = source == atom_ref[c].astype(F32)
        else:
            same = source == jnp.concatenate([edge_low] * 4, axis=1)
        rows.append(jnp.where(inside & jnp.broadcast_to(same, inside.shape), 1.0, 0.0))
    rows.append(jnp.zeros((3 * SLOT, 4 * LANES), F32))
    k_ref[...] = jnp.concatenate(rows, axis=0).T.astype(BF16)
    lower = coupling_ref[pl.ds(pl.multiple_of(place_ref[0] * ATOM_DEV, ATOM_DEV), ATOM_DEV), :]
    mine = coupling_ref[pl.ds(pl.multiple_of(place_ref[1] * ATOM_DEV, ATOM_DEV), ATOM_DEV), :]
    pair = jnp.concatenate([lower, mine], axis=0)
    pair = jnp.concatenate([pair, jnp.zeros((2 * ATOM_DEV, SLOT - NPROJ), F32)], axis=1)
    wide = jnp.concatenate([pair] * 8, axis=1)
    target = jnp.concatenate([own, jnp.where(which == 0, edge_low, -200.0)], axis=1)
    slot = row_iota(2 * ATOM_DEV, 2 * LANES).astype(F32)
    chosen = jnp.where(jnp.broadcast_to(target, slot.shape) == slot, wide, 0.0)
    coup_ref[...] = jnp.broadcast_to(jnp.sum(chosen, axis=0, keepdims=True), coup_ref.shape)
    low = padded_projectors(up_ref[16 : 16 + NPROJ, 0:NPC])
    stacked = jnp.concatenate([padded_projectors(proj_ref[:, 3, :]), low, jnp.zeros((2 * SLOT, NPC), F32)], axis=0)
    pe_ref[0], pe_ref[1] = split2(stacked.T)
    index_ref[...] = jnp.zeros_like(index_ref)
    index_ref[0:2, :] = maps_ref[0:2, :]
    sent = maps_ref[2:3, :]
    rows8 = [jnp.broadcast_to(b, (8, LANES)) for b in blocks_of(up_ref[41:42, 0:GHOST])]
    third = pick_row(rows8, sent)
    third = jnp.where(jnp.broadcast_to(sent, third.shape) >= 0, third, -1.0)[0:1].astype(jnp.int32)
    index_ref[2:3, :] = third
    index_ref[3:4, 0:NPC] = up_ref[40:41, 0:NPC].astype(jnp.int32) - NODES
    spread = jnp.concatenate([pn_ref[...], pick_row(blocks_of(low), third), jnp.zeros((3 * SLOT, NODES), F32)], axis=0)
    p_ref[0], p_ref[1] = split2(spread)


def inner_kernel(mode, v_ref, prev_ref, conn_ref, maps_ref, pot_ref, e_ref, base_ref):
    v = v_ref[...]
    sources = blocks_of(v)
    cells = [pick_row(sources, conn_ref[c : c + 1, :]) for c in range(3)]
    x_high, x_low = split2(jnp.concatenate(cells, axis=0))
    y = product(x_high, x_low, e_ref[0], e_ref[1])
    blocks = []
    for c in range(3):
        blocks += blocks_of(y[c * BANDS : (c + 1) * BANDS])
    for k in range(NODES // LANES):
        here = slice(k * LANES, (k + 1) * LANES)
        h = pick(blocks, maps_ref[0:1, here]) + pick(blocks, maps_ref[1:2, here]) + pot_ref[:, here] * v[:, here]
        if mode == "first":
            h = (h - CENTER * v[:, here]) * (1.0 / HALF_WIDTH)
        elif mode == "middle":
            h = (h - CENTER * v[:, here]) * (2.0 / HALF_WIDTH) - prev_ref[:, here]
        base_ref[:, here] = h


def outer(ups_ref, downs_ref, up_ref, down_ref, conn_ref, index_ref, e_ref, p_ref, pe_ref, k_ref, coup_ref):
    edge = ups_ref[0:BANDS, 0:NPC] + pick_row(blocks_of(down_ref[0:BANDS, 0:GHOST]), conn_ref[3:4, :] - NODES)
    low = up_ref[0:BANDS, 0:NPC] + pick_row(blocks_of(downs_ref[0:BANDS, 0:GHOST]), index_ref[3:4, 0:NPC])
    x_high, x_low = split2(jnp.concatenate([edge, low], axis=0))
    wide = product(x_high, x_low, pe_ref[0], pe_ref[1])
    which = lane_iota(BANDS, LANES) >> 5
    edges = jnp.where(which == 0, wide[:BANDS], jnp.where(which == 1, wide[BANDS:], 0.0))
    partials = jnp.concatenate([ups_ref[0:BANDS, NPC:], edges, down_ref[0:BANDS, GHOST:], up_ref[0:BANDS, NPC:]], axis=1)
    sums = dot(jnp.concatenate(split3(partials), axis=0), k_ref[...])
    w_high, w_low = split2((sums[0:16] + sums[16:32] + sums[32:48]) * coup_ref[0:1, :])
    nonlocal_part = product(w_high, w_low, p_ref[0], p_ref[1])
    y = product(x_high, x_low, e_ref[0], e_ref[1])
    own, other = blocks_of(y[:BANDS]), blocks_of(y[BANDS:])
    out = []
    for k in range(NODES // LANES):
        here = slice(k * LANES, (k + 1) * LANES)
        total = pick(own, index_ref[0:1, here], 12) + pick(own, index_ref[1:2, here], 12)
        out.append(total + pick(other, index_ref[2:3, here]))
    return jnp.concatenate(out, axis=1) + nonlocal_part


def outer_kernel(factor, base_ref, ups_ref, downs_ref, up_ref, down_ref, conn_ref, index_ref, e_ref, p_ref, pe_ref, k_ref, coup_ref,
                 send_ref, pt_ref, new_ref, upo_ref, downo_ref):
    h = outer(ups_ref, downs_ref, up_ref, down_ref, conn_ref, index_ref, e_ref, p_ref, pe_ref, k_ref, coup_ref)
    new = base_ref[...] + h * factor
    new_ref[...] = new
    v_high, v_low = split2(new)
    pack_message(new, product(v_high, v_low, pt_ref[0], pt_ref[1]), conn_ref, send_ref, upo_ref, downo_ref)


def gram_kernel(base_ref, ups_ref, downs_ref, up_ref, down_ref, conn_ref, index_ref, e_ref, p_ref, pe_ref, k_ref, coup_ref,
                v_ref, all_ref, out_ref):
    h = base_ref[...] + outer(ups_ref, downs_ref, up_ref, down_ref, conn_ref, index_ref, e_ref, p_ref, pe_ref, k_ref, coup_ref)
    s_high, s_low = split2(jnp.concatenate([h, v_ref[...]], axis=0))
    a_high, a_low = split2(all_ref[...])
    both = dot_nt(jnp.concatenate([s_high, s_low], axis=0), a_high)
    panel = both[:32] + both[32:] + dot_nt(s_high, a_low)
    for i in range(out_ref.shape[0]):
        out_ref[i] = panel


def add_kernel(parts_ref, out_ref):
    total = parts_ref[0]
    for i in range(1, parts_ref.shape[0]):
        total = total + parts_ref[i]
    for i in range(out_ref.shape[0]):
        out_ref[i] = total


def last_kernel(scale, parts_ref, projected_ref, correlation_ref):
    total = parts_ref[0]
    for i in range(1, parts_ref.shape[0]):
        total = total + parts_ref[i]
    projected_ref[...] = total[0:BANDS] * scale
    correlation_ref[...] = total[BANDS:] * scale


VM = pl.BlockSpec(memory_space=pltpu.VMEM)
SM = pl.BlockSpec(memory_space=pltpu.SMEM)


def call(kernel, outs, ins, *args):
    return pl.pallas_call(
        kernel,
        out_shape=[jax.ShapeDtypeStruct(s, t) for s, t in outs],
        in_specs=ins,
        out_specs=[VM] * len(outs),
        compiler_params=pltpu.CompilerParams(vmem_limit_bytes=40 * 2**20),
    )(*args)


def shifted(block, distance):
    size = lax.axis_size("fe")
    return lax.ppermute(block, "fe", [(i, (i + distance) % size) for i in range(size)])


def on_device(wavefunctions, potential, element_matrix, projectors, coupling, connectivity, send_list, atom_of_cell):
    fe_count = lax.axis_size("fe")
    fe = lax.axis_index("fe").astype(jnp.int32)
    place = jnp.stack([(fe + fe_count - 1) % fe_count, fe])
    send = send_list.reshape(1, GHOST)
    pot = potential.reshape(1, NODES)
    proj = projectors.transpose(1, 0, 2)
    ups, downs = call(
        first_kernel,
        [((48, 640), F32), ((24, 384), F32)],
        [VM, VM, VM, SM, VM],
        wavefunctions, connectivity, send, atom_of_cell, proj,
    )
    up = shifted(ups, 1)
    e, maps, pn, pt, downs = call(
        local_kernel,
        [((2, NPC, NPC), BF16), ((8, NODES), jnp.int32), ((4 * SLOT, NODES), F32), ((2, NODES, LANES), BF16), ((24, 384), F32)],
        [VM] * 5,
        connectivity, send, element_matrix, proj, downs,
    )
    down = shifted(downs, -1)

    def inner(mode, v, previous):
        return call(functools.partial(inner_kernel, mode), [((BANDS, NODES), F32)], [VM] * 6, v, previous, connectivity, maps, pot, e)[0]

    previous = current = wavefunctions
    base = inner("first", current, previous)
    p, pe, k, coup, index = call(
        joined_kernel,
        [((2, 256, NODES), BF16), ((2, NPC, LANES), BF16), ((512, 256), BF16), ((8, 256), F32), ((8, NODES), jnp.int32)],
        [VM, VM, VM, SM, SM, VM, VM, VM],
        up, down, maps, atom_of_cell, place, proj, coupling, pn,
    )
    shared = (connectivity, index, e, p, pe, k, coup)
    for step in range(DEGREE):
        last = step == DEGREE - 1
        new, ups, downs = call(
            functools.partial(outer_kernel, (1.0 if step == 0 else 2.0) / HALF_WIDTH),
            [((BANDS, NODES), F32), ((BANDS, 640), F32), ((BANDS, 384), F32)],
            [VM] * 14,
            base, ups, downs, up, down, *shared, send, pt,
        )
        previous, current = current, new
        if last:
            bands = lax.axis_size("band")
            everyone = lax.all_to_all(jnp.broadcast_to(current[None], (bands,) + current.shape), "band", 0, 0)
            everyone = everyone.reshape(-1, NODES)
        up, down = shifted(ups, 1), shifted(downs, -1)
        base = inner("last" if last else "middle", current, previous)
    (copies,) = call(
        gram_kernel,
        [((4, 32, LANES), F32)],
        [VM] * 14,
        base, ups, downs, up, down, *shared, current, everyone,
    )
    near = [[4 * i + j for j in range(4)] for i in range(fe_count // 4)]
    far = [[4 * i + j for i in range(fe_count // 4)] for j in range(4)]
    parts = lax.all_to_all(copies, "fe", 0, 0, axis_index_groups=near)
    (copies,) = call(add_kernel, [((fe_count // 4, 32, LANES), F32)], [VM], parts)
    parts = lax.all_to_all(copies, "fe", 0, 0, axis_index_groups=far)
    projected, correlation = call(
        functools.partial(last_kernel, 1.0 / (NODES * fe_count)),
        [((BANDS, LANES), F32), ((BANDS, LANES), F32)],
        [VM],
        parts,
    )
    return current, projected.T, correlation.T


def solution(mesh):
    in_specs = (
        P("band", "fe"),
        P("fe"),
        P(),
        P("fe", None, None),
        P(),
        P("fe", None),
        P("fe"),
        P("fe"),
    )
    out_specs = (P("band", "fe"), P(None, "band"), P(None, "band"))
    return jax.shard_map(on_device, mesh=mesh, in_specs=in_specs, out_specs=out_specs, check_vma=False)
```

```python
import functools

import jax
import jax.numpy as jnp
from jax import lax
from jax.experimental import pallas as pl
from jax.experimental.pallas import tpu as pltpu
from jax.sharding import PartitionSpec as P

NPROJ = 18
ATOM_DEV = 8
DEGREE = 6
CENTER = 0.9
HALF_WIDTH = 1.1
BANDS = 16
NODES = 1024
NPC = 512
GHOST = 256
LANES = 128
SLOT = 32
F32 = jnp.float32
BF16 = jnp.bfloat16


def dot(a, b):
    return lax.dot_general(a, b, (((1,), (0,)), ((), ())), preferred_element_type=F32)


def dot_nt(a, b):
    return lax.dot_general(a, b, (((1,), (1,)), ((), ())), preferred_element_type=F32)


def split2(x):
    high = x.astype(BF16)
    return high, (x - high.astype(F32)).astype(BF16)


def split3(x):
    high = x.astype(BF16)
    rest = x - high.astype(F32)
    mid = rest.astype(BF16)
    return high, mid, (rest - mid.astype(F32)).astype(BF16)


def product(x_high, x_low, w_high, w_low):
    rows = x_high.shape[0]
    both = dot(jnp.concatenate([x_high, x_low], axis=0), w_high)
    return both[:rows] + both[rows:] + dot(x_high, w_low)


def blocks_of(x):
    return [x[:, i : i + LANES] for i in range(0, x.shape[1], LANES)]


def pick(sources, index, first=0):
    rows = sources[0].shape[0]
    index = jnp.broadcast_to(index, (rows, LANES))
    lane = index & (LANES - 1)
    block = index >> 7
    total = jnp.zeros((rows, LANES), F32)
    for k, source in enumerate(sources):
        value = jnp.take_along_axis(source, lane, axis=1, mode="promise_in_bounds")
        total = jnp.where(block == first + k, value, total)
    return total


def pick_row(sources, index, first=0):
    return jnp.concatenate([pick(sources, i, first) for i in blocks_of(index)], axis=1)


def column(row):
    return jnp.broadcast_to(row, (LANES, row.shape[1])).T


def lane_iota(rows, lanes):
    return lax.broadcasted_iota(jnp.int32, (rows, lanes), 1)


def row_iota(rows, lanes):
    return lax.broadcasted_iota(jnp.int32, (rows, lanes), 0)


def padded_projectors(cell):
    return jnp.concatenate([cell, jnp.zeros((SLOT - NPROJ, NPC), F32)], axis=0)


def pack_message(vectors, partials, conn_ref, send_ref, up_ref, down_ref):
    sources = blocks_of(vectors)
    up_ref[0:BANDS, 0:NPC] = pick_row(sources, conn_ref[3:4, :])
    up_ref[0:BANDS, NPC:] = partials
    down_ref[0:BANDS, 0:GHOST] = pick_row(sources, send_ref[...])
    down_ref[0:BANDS, GHOST:] = partials


def first_kernel(v_ref, conn_ref, send_ref, atom_ref, proj_ref, pot_ref, coupling_ref, up_ref, down_ref):
    v = v_ref[...]
    sources = blocks_of(v)
    cells = [pick_row(sources, conn_ref[c : c + 1, :]) for c in range(3)]
    stacked = [padded_projectors(proj_ref[c]) for c in range(3)] + [jnp.zeros((SLOT, NPC), F32)]
    t_high, t_low = split2(jnp.concatenate(stacked, axis=0).T)
    x_high, x_low = split2(jnp.concatenate(cells, axis=0))
    wide = product(x_high, x_low, t_high, t_low)
    which = lane_iota(BANDS, LANES) >> 5
    partials = jnp.zeros((BANDS, LANES), F32)
    for c in range(3):
        partials = jnp.where(which == c, wide[c * BANDS : (c + 1) * BANDS], partials)
    which = lane_iota(1, LANES) >> 5
    atoms = jnp.zeros((1, LANES), F32)
    for c in range(4):
        atoms = jnp.where(which == c, atom_ref[c].astype(F32), atoms)
    edge = conn_ref[3:4, :]
    names = column(edge.astype(F32))
    position = row_iota(NPC, LANES).astype(F32)
    inverse = []
    for k in range(GHOST // LANES):
        slot = (lane_iota(NPC, LANES) + (NODES + k * LANES)).astype(F32)
        inverse.append(jnp.max(jnp.where(names == slot, position, -1.0), axis=0, keepdims=True))
    up_ref[...] = jnp.zeros_like(up_ref)
    down_ref[...] = jnp.zeros_like(down_ref)
    pack_message(v, partials, conn_ref, send_ref, up_ref, down_ref)
    up_ref[16 : 16 + NPROJ, 0:NPC] = proj_ref[3]
    up_ref[40:41, 0:NPC] = edge.astype(F32)
    up_ref[41:42, 0:GHOST] = jnp.concatenate(inverse, axis=1)
    up_ref[42:43, 0:LANES] = atoms
    down_ref[16:17, 0:LANES] = atoms


def local_kernel(conn_ref, send_ref, element_ref, proj_ref, down_ref, e_ref, maps_ref, p_ref, pt_ref, downo_ref):
    downo_ref[...] = down_ref[...]
    high, low = split2(element_ref[...])
    e_ref[0] = high
    e_ref[1] = low
    least = [jnp.full((1, LANES), 4.0 * NPC, F32)] * (NODES // LANES)
    most = [jnp.full((1, LANES), -1.0, F32)] * (NODES // LANES)
    position = row_iota(NPC, LANES).astype(F32)
    node = lane_iota(NPC, LANES).astype(F32)
    for c in range(4):
        names = column(conn_ref[c : c + 1, :].astype(F32))
        place = position + float(c * NPC)
        thirds = jnp.concatenate(split3(padded_projectors(proj_ref[c])), axis=0)
        for k in range(0, NODES // LANES, 2):
            hits = []
            for j in (k, k + 1):
                same = names == node + float(j * LANES)
                least[j] = jnp.minimum(least[j], jnp.min(jnp.where(same, place, 4.0 * NPC), axis=0, keepdims=True))
                most[j] = jnp.maximum(most[j], jnp.max(jnp.where(same, place, -1.0), axis=0, keepdims=True))
                hits.append(jnp.where(same, 1.0, 0.0).astype(BF16))
            parts = dot(thirds, jnp.concatenate(hits, axis=1))
            p_ref[c * SLOT : (c + 1) * SLOT, k * LANES : (k + 2) * LANES] = parts[:SLOT] + parts[SLOT : 2 * SLOT] + parts[2 * SLOT :]
    inner = jnp.concatenate([p_ref[0 : 3 * SLOT, :], jnp.zeros((SLOT, NODES), F32)], axis=0)
    pt_ref[0], pt_ref[1] = split2(inner.T)
    names = column(send_ref[...].astype(F32))
    maps_ref[...] = jnp.zeros_like(maps_ref)
    for k in range(NODES // LANES):
        here = slice(k * LANES, (k + 1) * LANES)
        maps_ref[0:1, here] = least[k].astype(jnp.int32)
        maps_ref[1:2, here] = jnp.where(most[k] > least[k], most[k], -1.0).astype(jnp.int32)
        same = names == node[:GHOST] + float(k * LANES)
        maps_ref[2:3, here] = jnp.max(jnp.where(same, position[:GHOST], -1.0), axis=0, keepdims=True).astype(jnp.int32)


def joined_kernel(up_ref, down_ref, maps_ref, atom_ref, proj_ref, coupling_ref, pn_ref, p_ref, pe_ref, k_ref, index_ref):
    low_atoms, high_atoms = up_ref[42:43, 0:LANES], down_ref[16:17, 0:LANES]
    which = lane_iota(1, LANES) >> 5
    own = jnp.full((1, LANES), -100.0, F32)
    for c in range(4):
        own = jnp.where(which == c, atom_ref[c].astype(F32), own)
    edge_low = jnp.broadcast_to(low_atoms[:, 96:97] - float(ATOM_DEV), (1, LANES))
    edges = jnp.where(which == 0, atom_ref[3].astype(F32), jnp.where(which == 1, edge_low, -200.0))
    from_upper = jnp.where(which < 3, high_atoms + float(ATOM_DEV), -300.0)
    from_lower = jnp.where(which < 3, low_atoms - float(ATOM_DEV), -400.0)
    source = jnp.concatenate([jnp.where(which < 3, own, -500.0), edges, from_upper, from_lower], axis=1)
    inside = (lane_iota(SLOT, 4 * LANES) & (SLOT - 1)) == row_iota(SLOT, 4 * LANES)
    rows = []
    for c in range(5):
        if c < 4:
            same = source == atom_ref[c].astype(F32)
        else:
            same = source == jnp.concatenate([edge_low] * 4, axis=1)
        rows.append(jnp.where(inside & jnp.broadcast_to(same, inside.shape), 1.0, 0.0))
    rows.append(jnp.zeros((3 * SLOT, 4 * LANES), F32))
    k_ref[...] = jnp.concatenate(rows, axis=0).T.astype(BF16)
    low = padded_projectors(up_ref[16 : 16 + NPROJ, 0:NPC])
    stacked = jnp.concatenate([padded_projectors(proj_ref[3]), low, jnp.zeros((2 * SLOT, NPC), F32)], axis=0)
    pe_ref[0], pe_ref[1] = split2(stacked.T)
    index_ref[...] = jnp.zeros_like(index_ref)
    index_ref[0:2, :] = maps_ref[0:2, :]
    sent = maps_ref[2:3, :]
    rows8 = [jnp.broadcast_to(b, (8, LANES)) for b in blocks_of(up_ref[41:42, 0:GHOST])]
    third = pick_row(rows8, sent)
    third = jnp.where(jnp.broadcast_to(sent, third.shape) >= 0, third, -1.0)[0:1].astype(jnp.int32)
    index_ref[2:3, :] = third
    index_ref[3:4, 0:NPC] = up_ref[40:41, 0:NPC].astype(jnp.int32) - NODES
    size = lax.axis_size("fe")
    fe = lax.axis_index("fe")
    below = lax.rem(fe + size - 1, size)
    row = lane_iota(1, coupling_ref.shape[1])
    offset = row - below * ATOM_DEV
    slots = jnp.where((offset >= 0) & (offset < ATOM_DEV), offset, -600)
    offset = row - fe * ATOM_DEV
    slots = jnp.where((offset >= 0) & (offset < ATOM_DEV), offset + ATOM_DEV, slots).astype(F32)
    factors = []
    for c in range(5):
        name = atom_ref[c].astype(F32) if c < 4 else jnp.broadcast_to(edge_low[:, 0:1], slots.shape)
        mine = jnp.where(jnp.broadcast_to(slots == name, coupling_ref.shape), coupling_ref[...], 0.0)
        factors.append(jnp.sum(mine, axis=1, keepdims=True))
        factors.append(jnp.zeros((SLOT - NPROJ, 1), F32))
    spread = jnp.concatenate([pn_ref[...], pick_row(blocks_of(low), third)], axis=0) * jnp.concatenate(factors, axis=0)
    spread = jnp.concatenate([spread, jnp.zeros((3 * SLOT, NODES), F32)], axis=0)
    p_ref[0], p_ref[1] = split2(spread)


def inner_kernel(mode, v_ref, prev_ref, conn_ref, maps_ref, pot_ref, e_ref, base_ref):
    v = v_ref[...]
    sources = blocks_of(v)
    cells = [pick_row(sources, conn_ref[c : c + 1, :]) for c in range(3)]
    x_high, x_low = split2(jnp.concatenate(cells, axis=0))
    y = product(x_high, x_low, e_ref[0], e_ref[1])
    blocks = []
    for c in range(3):
        blocks += blocks_of(y[c * BANDS : (c + 1) * BANDS])
    for k in range(NODES // LANES):
        here = slice(k * LANES, (k + 1) * LANES)
        h = pick(blocks, maps_ref[0:1, here]) + pick(blocks, maps_ref[1:2, here]) + pot_ref[:, here] * v[:, here]
        if mode == "first":
            h = (h - CENTER * v[:, here]) * (1.0 / HALF_WIDTH)
        elif mode == "middle":
            h = (h - CENTER * v[:, here]) * (2.0 / HALF_WIDTH) - prev_ref[:, here]
        base_ref[:, here] = h


def outer(ups_ref, downs_ref, up_ref, down_ref, conn_ref, index_ref, e_ref, p_ref, pe_ref, k_ref):
    edge = ups_ref[0:BANDS, 0:NPC] + pick_row(blocks_of(down_ref[0:BANDS, 0:GHOST]), conn_ref[3:4, :] - NODES)
    low = up_ref[0:BANDS, 0:NPC] + pick_row(blocks_of(downs_ref[0:BANDS, 0:GHOST]), index_ref[3:4, 0:NPC])
    x_high, x_low = split2(jnp.concatenate([edge, low], axis=0))
    wide = product(x_high, x_low, pe_ref[0], pe_ref[1])
    which = lane_iota(BANDS, LANES) >> 5
    edges = jnp.where(which == 0, wide[:BANDS], jnp.where(which == 1, wide[BANDS:], 0.0))
    partials = jnp.concatenate([ups_ref[0:BANDS, NPC:], edges, down_ref[0:BANDS, GHOST:], up_ref[0:BANDS, NPC:]], axis=1)
    sums = dot(jnp.concatenate(split3(partials), axis=0), k_ref[...])
    w_high, w_low = split2(sums[0:16] + sums[16:32] + sums[32:48])
    nonlocal_part = product(w_high, w_low, p_ref[0], p_ref[1])
    y = product(x_high, x_low, e_ref[0], e_ref[1])
    own, other = blocks_of(y[:BANDS]), blocks_of(y[BANDS:])
    out = []
    for k in range(NODES // LANES):
        here = slice(k * LANES, (k + 1) * LANES)
        total = pick(own, index_ref[0:1, here], 12) + pick(own, index_ref[1:2, here], 12)
        out.append(total + pick(other, index_ref[2:3, here]))
    return jnp.concatenate(out, axis=1) + nonlocal_part


def outer_kernel(factor, base_ref, ups_ref, downs_ref, up_ref, down_ref, conn_ref, index_ref, e_ref, p_ref, pe_ref, k_ref,
                 send_ref, pt_ref, new_ref, upo_ref, downo_ref, *copies_ref):
    h = outer(ups_ref, downs_ref, up_ref, down_ref, conn_ref, index_ref, e_ref, p_ref, pe_ref, k_ref)
    new = base_ref[...] + h * factor
    new_ref[...] = new
    for ref in copies_ref:
        for i in range(ref.shape[0]):
            ref[i] = new
    v_high, v_low = split2(new)
    pack_message(new, product(v_high, v_low, pt_ref[0], pt_ref[1]), conn_ref, send_ref, upo_ref, downo_ref)


def gram_kernel(base_ref, ups_ref, downs_ref, up_ref, down_ref, conn_ref, index_ref, e_ref, p_ref, pe_ref, k_ref,
                v_ref, all_ref, out_ref):
    h = base_ref[...] + outer(ups_ref, downs_ref, up_ref, down_ref, conn_ref, index_ref, e_ref, p_ref, pe_ref, k_ref)
    s_high, s_low = split2(jnp.concatenate([h, v_ref[...]], axis=0))
    a_high, a_low = split2(all_ref[...])
    both = dot_nt(jnp.concatenate([s_high, s_low], axis=0), a_high)
    panel = both[:32] + both[32:] + dot_nt(s_high, a_low)
    for i in range(out_ref.shape[0]):
        out_ref[i] = panel


def add_kernel(parts_ref, out_ref):
    total = parts_ref[0]
    for i in range(1, parts_ref.shape[0]):
        total = total + parts_ref[i]
    for i in range(out_ref.shape[0]):
        out_ref[i] = total


def last_kernel(scale, parts_ref, projected_ref, correlation_ref):
    total = parts_ref[0]
    for i in range(1, parts_ref.shape[0]):
        total = total + parts_ref[i]
    projected_ref[...] = total[0:BANDS] * scale
    correlation_ref[...] = total[BANDS:] * scale


VM = pl.BlockSpec(memory_space=pltpu.VMEM)
SM = pl.BlockSpec(memory_space=pltpu.SMEM)


def call(kernel, outs, ins, *args):
    return pl.pallas_call(
        kernel,
        out_shape=[jax.ShapeDtypeStruct(s, t) for s, t in outs],
        in_specs=ins,
        out_specs=[VM] * len(outs),
        compiler_params=pltpu.CompilerParams(vmem_limit_bytes=24 * 2**20),
    )(*args)


def shifted(block, distance):
    size = lax.axis_size("fe")
    return lax.ppermute(block, "fe", [(i, (i + distance) % size) for i in range(size)])


def on_device(wavefunctions, potential, element_matrix, projectors, coupling, connectivity, send_list, atom_of_cell):
    fe_count = lax.axis_size("fe")
    v, conn, send = wavefunctions, connectivity, send_list.reshape(1, GHOST)
    pot, couple = potential.reshape(1, NODES), coupling.T
    ups, downs = call(
        first_kernel,
        [((48, 640), F32), ((24, 384), F32)],
        [VM, VM, VM, SM, VM, VM, VM],
        v, conn, send, atom_of_cell, projectors, pot, couple,
    )
    up = shifted(ups, 1)
    e, maps, pn, pt, downs = call(
        local_kernel,
        [((2, NPC, NPC), BF16), ((8, NODES), jnp.int32), ((4 * SLOT, NODES), F32), ((2, NODES, LANES), BF16), ((24, 384), F32)],
        [VM] * 5,
        conn, send, element_matrix, projectors, downs,
    )
    down = shifted(downs, -1)

    def inner(mode, v, previous):
        return call(functools.partial(inner_kernel, mode), [((BANDS, NODES), F32)], [VM] * 6, v, previous, conn, maps, pot, e)[0]

    previous = current = v
    base = inner("first", current, previous)
    p, pe, k, index = call(
        joined_kernel,
        [((2, 256, NODES), BF16), ((2, NPC, LANES), BF16), ((512, 256), BF16), ((8, NODES), jnp.int32)],
        [VM, VM, VM, SM, VM, VM, VM],
        up, down, maps, atom_of_cell, projectors, couple, pn,
    )
    shared = (conn, index, e, p, pe, k)
    for step in range(DEGREE):
        last = step == DEGREE - 1
        copied = [((lax.axis_size("band"), BANDS, NODES), F32)] if last else []
        new, ups, downs, *copied = call(
            functools.partial(outer_kernel, (1.0 if step == 0 else 2.0) / HALF_WIDTH),
            [((BANDS, NODES), F32), ((BANDS, 640), F32), ((BANDS, 384), F32)] + copied,
            [VM] * 13,
            base, ups, downs, up, down, *shared, send, pt,
        )
        previous, current = current, new
        if last:
            everyone = lax.all_to_all(copied[0], "band", 0, 0).reshape(-1, NODES)
        up, down = shifted(ups, 1), shifted(downs, -1)
        base = inner("last" if last else "middle", current, previous)
    (copies,) = call(
        gram_kernel,
        [((4, 32, LANES), F32)],
        [VM] * 13,
        base, ups, downs, up, down, *shared, current, everyone,
    )
    near = [[4 * i + j for j in range(4)] for i in range(fe_count // 4)]
    far = [[4 * i + j for i in range(fe_count // 4)] for j in range(4)]
    parts = lax.all_to_all(copies, "fe", 0, 0, axis_index_groups=near)
    (copies,) = call(add_kernel, [((fe_count // 4, 32, LANES), F32)], [VM], parts)
    parts = lax.all_to_all(copies, "fe", 0, 0, axis_index_groups=far)
    projected, correlation = call(
        functools.partial(last_kernel, 1.0 / (NODES * fe_count)),
        [((BANDS, LANES), F32), ((BANDS, LANES), F32)],
        [VM],
        parts,
    )
    return current, projected.T, correlation.T


def solution(mesh):
    in_specs = (
        P("band", "fe"),
        P("fe"),
        P(),
        P("fe", None, None),
        P(),
        P("fe", None),
        P("fe"),
        P("fe"),
    )
    out_specs = (P("band", "fe"), P(None, "band"), P(None, "band"))
    return jax.shard_map(on_device, mesh=mesh, in_specs=in_specs, out_specs=out_specs, check_vma=False)
```

```python
import functools

import jax
import jax.numpy as jnp
from jax import lax
from jax.experimental import pallas as pl
from jax.experimental.pallas import tpu as pltpu
from jax.sharding import PartitionSpec as P

NPROJ = 18
ATOM_DEV = 8
DEGREE = 6
CENTER = 0.9
HALF_WIDTH = 1.1
BANDS = 16
NODES = 1024
NPC = 512
GHOST = 256
LANES = 128
SLOT = 32
F32 = jnp.float32
BF16 = jnp.bfloat16


def dot(a, b):
    return lax.dot_general(a, b, (((1,), (0,)), ((), ())), preferred_element_type=F32)


def dot_nt(a, b):
    return lax.dot_general(a, b, (((1,), (1,)), ((), ())), preferred_element_type=F32)


def split2(x):
    high = x.astype(BF16)
    return high, (x - high.astype(F32)).astype(BF16)


def split3(x):
    high = x.astype(BF16)
    rest = x - high.astype(F32)
    mid = rest.astype(BF16)
    return high, mid, (rest - mid.astype(F32)).astype(BF16)


def product(x_high, x_low, w_high, w_low):
    rows = x_high.shape[0]
    both = dot(jnp.concatenate([x_high, x_low], axis=0), w_high)
    return both[:rows] + both[rows:] + dot(x_high, w_low)


def blocks_of(x):
    return [x[:, i : i + LANES] for i in range(0, x.shape[1], LANES)]


def pick(sources, index, first=0):
    rows = sources[0].shape[0]
    index = jnp.broadcast_to(index, (rows, LANES))
    lane = index & (LANES - 1)
    block = index >> 7
    total = jnp.zeros((rows, LANES), F32)
    for k, source in enumerate(sources):
        value = jnp.take_along_axis(source, lane, axis=1, mode="promise_in_bounds")
        total = jnp.where(block == first + k, value, total)
    return total


def pick_row(sources, index, first=0):
    return jnp.concatenate([pick(sources, i, first) for i in blocks_of(index)], axis=1)


def column(row):
    return jnp.broadcast_to(row, (LANES, row.shape[1])).T


def lane_iota(rows, lanes):
    return lax.broadcasted_iota(jnp.int32, (rows, lanes), 1)


def row_iota(rows, lanes):
    return lax.broadcasted_iota(jnp.int32, (rows, lanes), 0)


def padded_projectors(cell):
    return jnp.concatenate([cell, jnp.zeros((SLOT - NPROJ, NPC), F32)], axis=0)


def pack_message(vectors, partials, conn_ref, send_ref, up_ref, down_ref):
    sources = blocks_of(vectors)
    up_ref[0:BANDS, 0:NPC] = pick_row(sources, conn_ref[3:4, :])
    up_ref[0:BANDS, NPC:] = partials
    down_ref[0:BANDS, 0:GHOST] = pick_row(sources, send_ref[...])
    down_ref[0:BANDS, GHOST:] = partials


def first_kernel(v_ref, conn_ref, send_ref, atom_ref, proj_ref, pot_ref, coupling_ref, up_ref, down_ref):
    v = v_ref[...]
    sources = blocks_of(v)
    cells = [pick_row(sources, conn_ref[c : c + 1, :]) for c in range(3)]
    stacked = [padded_projectors(proj_ref[c]) for c in range(3)] + [jnp.zeros((SLOT, NPC), F32)]
    t_high, t_low = split2(jnp.concatenate(stacked, axis=0).T)
    x_high, x_low = split2(jnp.concatenate(cells, axis=0))
    wide = product(x_high, x_low, t_high, t_low)
    which = lane_iota(BANDS, LANES) >> 5
    partials = jnp.zeros((BANDS, LANES), F32)
    for c in range(3):
        partials = jnp.where(which == c, wide[c * BANDS : (c + 1) * BANDS], partials)
    which = lane_iota(1, LANES) >> 5
    atoms = jnp.zeros((1, LANES), F32)
    for c in range(4):
        atoms = jnp.where(which == c, atom_ref[c].astype(F32), atoms)
    edge = conn_ref[3:4, :]
    names = column(edge.astype(F32))
    position = row_iota(NPC, LANES).astype(F32)
    inverse = []
    for k in range(GHOST // LANES):
        slot = (lane_iota(NPC, LANES) + (NODES + k * LANES)).astype(F32)
        inverse.append(jnp.max(jnp.where(names == slot, position, -1.0), axis=0, keepdims=True))
    up_ref[...] = jnp.zeros_like(up_ref)
    down_ref[...] = jnp.zeros_like(down_ref)
    pack_message(v, partials, conn_ref, send_ref, up_ref, down_ref)
    up_ref[16 : 16 + NPROJ, 0:NPC] = proj_ref[3]
    up_ref[40:41, 0:NPC] = edge.astype(F32)
    up_ref[41:42, 0:GHOST] = jnp.concatenate(inverse, axis=1)
    up_ref[42:43, 0:LANES] = atoms
    down_ref[16:17, 0:LANES] = atoms


def split_kernel(x_ref, out_ref):
    out_ref[0], out_ref[1] = split2(x_ref[...])


def local_kernel(conn_ref, send_ref, proj_ref, maps_ref, p_ref, pt_ref):
    least = [jnp.full((1, LANES), 4.0 * NPC, F32)] * (NODES // LANES)
    most = [jnp.full((1, LANES), -1.0, F32)] * (NODES // LANES)
    position = row_iota(NPC, LANES).astype(F32)
    node = lane_iota(NPC, LANES).astype(F32)
    for c in range(4):
        names = column(conn_ref[c : c + 1, :].astype(F32))
        place = position + float(c * NPC)
        thirds = jnp.concatenate(split3(padded_projectors(proj_ref[c])), axis=0)
        for k in range(0, NODES // LANES, 2):
            hits = []
            for j in (k, k + 1):
                same = names == node + float(j * LANES)
                least[j] = jnp.minimum(least[j], jnp.min(jnp.where(same, place, 4.0 * NPC), axis=0, keepdims=True))
                most[j] = jnp.maximum(most[j], jnp.max(jnp.where(same, place, -1.0), axis=0, keepdims=True))
                hits.append(jnp.where(same, 1.0, 0.0).astype(BF16))
            parts = dot(thirds, jnp.concatenate(hits, axis=1))
            p_ref[c * SLOT : (c + 1) * SLOT, k * LANES : (k + 2) * LANES] = parts[:SLOT] + parts[SLOT : 2 * SLOT] + parts[2 * SLOT :]
    inner = jnp.concatenate([p_ref[0 : 3 * SLOT, :], jnp.zeros((SLOT, NODES), F32)], axis=0)
    pt_ref[0], pt_ref[1] = split2(inner.T)
    names = column(send_ref[...].astype(F32))
    maps_ref[...] = jnp.zeros_like(maps_ref)
    for k in range(NODES // LANES):
        here = slice(k * LANES, (k + 1) * LANES)
        maps_ref[0:1, here] = least[k].astype(jnp.int32)
        maps_ref[1:2, here] = jnp.where(most[k] > least[k], most[k], -1.0).astype(jnp.int32)
        same = names == node[:GHOST] + float(k * LANES)
        maps_ref[2:3, here] = jnp.max(jnp.where(same, position[:GHOST], -1.0), axis=0, keepdims=True).astype(jnp.int32)


def joined_kernel(up_ref, down_ref, maps_ref, atom_ref, proj_ref, coupling_ref, pn_ref, p_ref, pe_ref, k_ref, index_ref):
    low_atoms, high_atoms = up_ref[42:43, 0:LANES], down_ref[16:17, 0:LANES]
    which = lane_iota(1, LANES) >> 5
    own = jnp.full((1, LANES), -100.0, F32)
    for c in range(4):
        own = jnp.where(which == c, atom_ref[c].astype(F32), own)
    edge_low = jnp.broadcast_to(low_atoms[:, 96:97] - float(ATOM_DEV), (1, LANES))
    edges = jnp.where(which == 0, atom_ref[3].astype(F32), jnp.where(which == 1, edge_low, -200.0))
    from_upper = jnp.where(which < 3, high_atoms + float(ATOM_DEV), -300.0)
    from_lower = jnp.where(which < 3, low_atoms - float(ATOM_DEV), -400.0)
    source = jnp.concatenate([jnp.where(which < 3, own, -500.0), edges, from_upper, from_lower], axis=1)
    inside = (lane_iota(SLOT, 4 * LANES) & (SLOT - 1)) == row_iota(SLOT, 4 * LANES)
    rows = []
    for c in range(5):
        if c < 4:
            same = source == atom_ref[c].astype(F32)
        else:
            same = source == jnp.concatenate([edge_low] * 4, axis=1)
        rows.append(jnp.where(inside & jnp.broadcast_to(same, inside.shape), 1.0, 0.0))
    rows.append(jnp.zeros((3 * SLOT, 4 * LANES), F32))
    k_ref[...] = jnp.concatenate(rows, axis=0).T.astype(BF16)
    low = padded_projectors(up_ref[16 : 16 + NPROJ, 0:NPC])
    stacked = jnp.concatenate([padded_projectors(proj_ref[3]), low, jnp.zeros((2 * SLOT, NPC), F32)], axis=0)
    pe_ref[0], pe_ref[1] = split2(stacked.T)
    index_ref[...] = jnp.zeros_like(index_ref)
    index_ref[0:2, :] = maps_ref[0:2, :]
    sent = maps_ref[2:3, :]
    rows8 = [jnp.broadcast_to(b, (8, LANES)) for b in blocks_of(up_ref[41:42, 0:GHOST])]
    third = pick_row(rows8, sent)
    third = jnp.where(jnp.broadcast_to(sent, third.shape) >= 0, third, -1.0)[0:1].astype(jnp.int32)
    index_ref[2:3, :] = third
    index_ref[3:4, 0:NPC] = up_ref[40:41, 0:NPC].astype(jnp.int32) - NODES
    size = lax.axis_size("fe")
    fe = lax.axis_index("fe")
    below = lax.rem(fe + size - 1, size)
    row = lane_iota(1, coupling_ref.shape[1])
    offset = row - below * ATOM_DEV
    slots = jnp.where((offset >= 0) & (offset < ATOM_DEV), offset, -600)
    offset = row - fe * ATOM_DEV
    slots = jnp.where((offset >= 0) & (offset < ATOM_DEV), offset + ATOM_DEV, slots).astype(F32)
    factors = []
    for c in range(5):
        name = atom_ref[c].astype(F32) if c < 4 else jnp.broadcast_to(edge_low[:, 0:1], slots.shape)
        mine = jnp.where(jnp.broadcast_to(slots == name, coupling_ref.shape), coupling_ref[...], 0.0)
        factors.append(jnp.sum(mine, axis=1, keepdims=True))
        factors.append(jnp.zeros((SLOT - NPROJ, 1), F32))
    spread = jnp.concatenate([pn_ref[...], pick_row(blocks_of(low), third)], axis=0) * jnp.concatenate(factors, axis=0)
    spread = jnp.concatenate([spread, jnp.zeros((3 * SLOT, NODES), F32)], axis=0)
    p_ref[0], p_ref[1] = split2(spread)


def inner_kernel(mode, v_ref, prev_ref, conn_ref, maps_ref, pot_ref, e_ref, base_ref, *result_ref):
    v = v_ref[...]
    for ref in result_ref:
        ref[...] = v
    sources = blocks_of(v)
    cells = [pick_row(sources, conn_ref[c : c + 1, :]) for c in range(3)]
    x_high, x_low = split2(jnp.concatenate(cells, axis=0))
    y = product(x_high, x_low, e_ref[0], e_ref[1])
    blocks = []
    for c in range(3):
        blocks += blocks_of(y[c * BANDS : (c + 1) * BANDS])
    for k in range(NODES // LANES):
        here = slice(k * LANES, (k + 1) * LANES)
        h = pick(blocks, maps_ref[0:1, here]) + pick(blocks, maps_ref[1:2, here]) + pot_ref[:, here] * v[:, here]
        if mode == "first":
            h = (h - CENTER * v[:, here]) * (1.0 / HALF_WIDTH)
        elif mode == "middle":
            h = (h - CENTER * v[:, here]) * (2.0 / HALF_WIDTH) - prev_ref[:, here]
        base_ref[:, here] = h


def is_odd():
    return lax.rem(lax.axis_index("fe"), 2) == 1


def received(paired, one_ref, two_ref):
    if not paired:
        up, down = one_ref, two_ref
        return up[0:BANDS, 0:NPC], up[0:BANDS, NPC:], down[0:BANDS, 0:GHOST], down[0:BANDS, GHOST:]
    odd = is_odd()
    one, two = one_ref[...], two_ref[...]
    up, down = jnp.where(odd, two, one), jnp.where(odd, one[:, GHOST:], two[:, GHOST:])
    return up[:, 0:NPC], up[:, NPC:], down[:, 0:GHOST], down[:, GHOST:]


def outer(paired, ups_ref, downs_ref, one_ref, two_ref, conn_ref, index_ref, e_ref, p_ref, pe_ref, k_ref):
    from_lower, lower_partials, from_upper, upper_partials = received(paired, one_ref, two_ref)
    edge = ups_ref[0:BANDS, 0:NPC] + pick_row(blocks_of(from_upper), conn_ref[3:4, :] - NODES)
    low = from_lower + pick_row(blocks_of(downs_ref[0:BANDS, 0:GHOST]), index_ref[3:4, 0:NPC])
    x_high, x_low = split2(jnp.concatenate([edge, low], axis=0))
    wide = product(x_high, x_low, pe_ref[0], pe_ref[1])
    which = lane_iota(BANDS, LANES) >> 5
    edges = jnp.where(which == 0, wide[:BANDS], jnp.where(which == 1, wide[BANDS:], 0.0))
    partials = jnp.concatenate([ups_ref[0:BANDS, NPC:], edges, upper_partials, lower_partials], axis=1)
    sums = dot(jnp.concatenate(split3(partials), axis=0), k_ref[...])
    w_high, w_low = split2(sums[0:16] + sums[16:32] + sums[32:48])
    nonlocal_part = product(w_high, w_low, p_ref[0], p_ref[1])
    y = product(x_high, x_low, e_ref[0], e_ref[1])
    own, other = blocks_of(y[:BANDS]), blocks_of(y[BANDS:])
    out = []
    for k in range(NODES // LANES):
        here = slice(k * LANES, (k + 1) * LANES)
        total = pick(own, index_ref[0:1, here], 12) + pick(own, index_ref[1:2, here], 12)
        out.append(total + pick(other, index_ref[2:3, here]))
    return jnp.concatenate(out, axis=1) + nonlocal_part


def outer_kernel(paired, factor, base_ref, ups_ref, downs_ref, one_ref, two_ref, conn_ref, index_ref, e_ref, p_ref, pe_ref, k_ref,
                 send_ref, pt_ref, new_ref, upo_ref, downo_ref, oneo_ref, twoo_ref, *copies_ref):
    h = outer(paired, ups_ref, downs_ref, one_ref, two_ref, conn_ref, index_ref, e_ref, p_ref, pe_ref, k_ref)
    new = base_ref[...] + h * factor
    new_ref[...] = new
    for ref in copies_ref:
        for i in range(ref.shape[0]):
            ref[i] = new
    v_high, v_low = split2(new)
    pack_message(new, product(v_high, v_low, pt_ref[0], pt_ref[1]), conn_ref, send_ref, upo_ref, downo_ref)
    up = upo_ref[...]
    down = jnp.concatenate([jnp.zeros((BANDS, GHOST), F32), downo_ref[...]], axis=1)
    odd = is_odd()
    oneo_ref[...] = jnp.where(odd, up, down)
    twoo_ref[...] = jnp.where(odd, down, up)


def gram_kernel(base_ref, ups_ref, downs_ref, one_ref, two_ref, conn_ref, index_ref, e_ref, p_ref, pe_ref, k_ref,
                v_ref, all_ref, out_ref):
    h = base_ref[...] + outer(True, ups_ref, downs_ref, one_ref, two_ref, conn_ref, index_ref, e_ref, p_ref, pe_ref, k_ref)
    s_high, s_low = split2(jnp.concatenate([h, v_ref[...]], axis=0))
    a_high, a_low = split2(all_ref[...])
    both = dot_nt(jnp.concatenate([s_high, s_low], axis=0), a_high)
    panel = both[:32] + both[32:] + dot_nt(s_high, a_low)
    for i in range(out_ref.shape[0]):
        out_ref[i] = panel


def add_kernel(parts_ref, out_ref):
    total = parts_ref[0]
    for i in range(1, parts_ref.shape[0]):
        total = total + parts_ref[i]
    for i in range(out_ref.shape[0]):
        out_ref[i] = total


def last_kernel(scale, parts_ref, projected_ref, correlation_ref):
    total = parts_ref[0]
    for i in range(1, parts_ref.shape[0]):
        total = total + parts_ref[i]
    projected_ref[...] = total[0:BANDS] * scale
    correlation_ref[...] = total[BANDS:] * scale


VM = pl.BlockSpec(memory_space=pltpu.VMEM)
SM = pl.BlockSpec(memory_space=pltpu.SMEM)


def call(kernel, outs, ins, *args):
    return pl.pallas_call(
        kernel,
        out_shape=[jax.ShapeDtypeStruct(s, t) for s, t in outs],
        in_specs=ins,
        out_specs=[VM] * len(outs),
        compiler_params=pltpu.CompilerParams(vmem_limit_bytes=24 * 2**20),
    )(*args)


def shifted(block, distance):
    size = lax.axis_size("fe")
    return lax.ppermute(block, "fe", [(i, (i + distance) % size) for i in range(size)])


def swapped(block, first):
    size = lax.axis_size("fe")
    return lax.ppermute(block, "fe", [(i, (i + 1 if i % 2 == first else i - 1) % size) for i in range(size)])


def on_device(wavefunctions, potential, element_matrix, projectors, coupling, connectivity, send_list, atom_of_cell):
    fe_count = lax.axis_size("fe")
    v, conn, send = wavefunctions, connectivity, send_list.reshape(1, GHOST)
    pot, couple = potential.reshape(1, NODES), coupling.T
    ups, downs = call(
        first_kernel,
        [((48, 640), F32), ((24, 384), F32)],
        [VM, VM, VM, SM, VM, VM, VM],
        v, conn, send, atom_of_cell, projectors, pot, couple,
    )
    up, down = shifted(ups, 1), shifted(downs, -1)
    maps, pn, pt = call(
        local_kernel,
        [((8, NODES), jnp.int32), ((4 * SLOT, NODES), F32), ((2, NODES, LANES), BF16)],
        [VM] * 3,
        conn, send, projectors,
    )
    (e,) = call(split_kernel, [((2, NPC, NPC), BF16)], [VM], element_matrix)

    def inner(mode, v, previous):
        outs = [((BANDS, NODES), F32)] * (2 if mode == "last" else 1)
        return call(functools.partial(inner_kernel, mode), outs, [VM] * 6, v, previous, conn, maps, pot, e)

    previous = current = v
    (base,) = inner("first", current, previous)
    p, pe, k, index = call(
        joined_kernel,
        [((2, 256, NODES), BF16), ((2, NPC, LANES), BF16), ((512, 256), BF16), ((8, NODES), jnp.int32)],
        [VM, VM, VM, SM, VM, VM, VM],
        up, down, maps, atom_of_cell, projectors, couple, pn,
    )
    shared = (conn, index, e, p, pe, k)
    for step in range(DEGREE):
        last = step == DEGREE - 1
        copied = [((lax.axis_size("band"), BANDS, NODES), F32)] if last else []
        new, ups, downs, one, two, *copied = call(
            functools.partial(outer_kernel, step > 0, (1.0 if step == 0 else 2.0) / HALF_WIDTH),
            [((BANDS, NODES), F32), ((BANDS, 640), F32), ((BANDS, 384), F32), ((BANDS, 640), F32), ((BANDS, 640), F32)] + copied,
            [VM] * 13,
            base, ups, downs, up, down, *shared, send, pt,
        )
        previous, current = current, new
        if last:
            everyone = lax.all_to_all(copied[0], "band", 0, 0).reshape(-1, NODES)
        up, down = swapped(one, 1), swapped(two, 0)
        base, *result = inner("last" if last else "middle", current, current if last else previous)
    (copies,) = call(
        gram_kernel,
        [((4, 32, LANES), F32)],
        [VM] * 13,
        base, ups, downs, up, down, *shared, current, everyone,
    )
    near = [[4 * i + j for j in range(4)] for i in range(fe_count // 4)]
    far = [[4 * i + j for i in range(fe_count // 4)] for j in range(4)]
    parts = lax.all_to_all(copies, "fe", 0, 0, axis_index_groups=near)
    (copies,) = call(add_kernel, [((fe_count // 4, 32, LANES), F32)], [VM], parts)
    parts = lax.all_to_all(copies, "fe", 0, 0, axis_index_groups=far)
    projected, correlation = call(
        functools.partial(last_kernel, 1.0 / (NODES * fe_count)),
        [((BANDS, LANES), F32), ((BANDS, LANES), F32)],
        [VM],
        parts,
    )
    return result[0], projected.T, correlation.T


def solution(mesh):
    in_specs = (
        P("band", "fe"),
        P("fe"),
        P(),
        P("fe", None, None),
        P(),
        P("fe", None),
        P("fe"),
        P("fe"),
    )
    out_specs = (P("band", "fe"), P(None, "band"), P(None, "band"))
    return jax.shard_map(on_device, mesh=mesh, in_specs=in_specs, out_specs=out_specs, check_vma=False)
```

```python
import functools

import jax
import jax.numpy as jnp
from jax import lax
from jax.experimental import pallas as pl
from jax.experimental.pallas import tpu as pltpu
from jax.sharding import PartitionSpec as P

NPROJ = 18
ATOM_DEV = 8
DEGREE = 6
CENTER = 0.9
HALF_WIDTH = 1.1
BANDS = 16
NODES = 1024
NPC = 512
GHOST = 256
LANES = 128
SLOT = 32
F32 = jnp.float32
BF16 = jnp.bfloat16


def dot(a, b):
    return lax.dot_general(a, b, (((1,), (0,)), ((), ())), preferred_element_type=F32)


def dot_nt(a, b):
    return lax.dot_general(a, b, (((1,), (1,)), ((), ())), preferred_element_type=F32)


def split2(x):
    high = x.astype(BF16)
    return high, (x - high.astype(F32)).astype(BF16)


def split3(x):
    high = x.astype(BF16)
    rest = x - high.astype(F32)
    mid = rest.astype(BF16)
    return high, mid, (rest - mid.astype(F32)).astype(BF16)


def product(x_high, x_low, w_high, w_low):
    rows = x_high.shape[0]
    both = dot(jnp.concatenate([x_high, x_low], axis=0), w_high)
    return both[:rows] + both[rows:] + dot(x_high, w_low)


def blocks_of(x):
    return [x[:, i : i + LANES] for i in range(0, x.shape[1], LANES)]


def pick(sources, index, first=0):
    rows = sources[0].shape[0]
    index = jnp.broadcast_to(index, (rows, LANES))
    lane = index & (LANES - 1)
    block = index >> 7
    total = jnp.zeros((rows, LANES), F32)
    for k, source in enumerate(sources):
        value = jnp.take_along_axis(source, lane, axis=1, mode="promise_in_bounds")
        total = jnp.where(block == first + k, value, total)
    return total


def pick_row(sources, index, first=0):
    return jnp.concatenate([pick(sources, i, first) for i in blocks_of(index)], axis=1)


def column(row):
    return jnp.broadcast_to(row, (LANES, row.shape[1])).T


def lane_iota(rows, lanes):
    return lax.broadcasted_iota(jnp.int32, (rows, lanes), 1)


def row_iota(rows, lanes):
    return lax.broadcasted_iota(jnp.int32, (rows, lanes), 0)


def padded_projectors(cell):
    return jnp.concatenate([cell, jnp.zeros((SLOT - NPROJ, NPC), F32)], axis=0)


def pack_message(vectors, partials, conn_ref, send_ref, up_ref, down_ref):
    sources = blocks_of(vectors)
    up_ref[0:BANDS, 0:NPC] = pick_row(sources, conn_ref[3:4, :])
    up_ref[0:BANDS, NPC:] = partials
    down_ref[0:BANDS, 0:GHOST] = pick_row(sources, send_ref[...])
    down_ref[0:BANDS, GHOST:] = partials


def first_kernel(v_ref, conn_ref, send_ref, atom_ref, proj_ref, pot_ref, coupling_ref, up_ref, down_ref):
    v = v_ref[...]
    sources = blocks_of(v)
    cells = [pick_row(sources, conn_ref[c : c + 1, :]) for c in range(3)]
    stacked = [padded_projectors(proj_ref[c]) for c in range(3)] + [jnp.zeros((SLOT, NPC), F32)]
    t_high, t_low = split2(jnp.concatenate(stacked, axis=0).T)
    x_high, x_low = split2(jnp.concatenate(cells, axis=0))
    wide = product(x_high, x_low, t_high, t_low)
    which = lane_iota(BANDS, LANES) >> 5
    partials = jnp.zeros((BANDS, LANES), F32)
    for c in range(3):
        partials = jnp.where(which == c, wide[c * BANDS : (c + 1) * BANDS], partials)
    which = lane_iota(1, LANES) >> 5
    atoms = jnp.zeros((1, LANES), F32)
    for c in range(4):
        atoms = jnp.where(which == c, atom_ref[c].astype(F32), atoms)
    edge = conn_ref[3:4, :]
    names = column(edge.astype(F32))
    position = row_iota(NPC, LANES).astype(F32)
    inverse = []
    for k in range(GHOST // LANES):
        slot = (lane_iota(NPC, LANES) + (NODES + k * LANES)).astype(F32)
        inverse.append(jnp.max(jnp.where(names == slot, position, -1.0), axis=0, keepdims=True))
    up_ref[...] = jnp.zeros_like(up_ref)
    down_ref[...] = jnp.zeros_like(down_ref)
    pack_message(v, partials, conn_ref, send_ref, up_ref, down_ref)
    up_ref[16 : 16 + NPROJ, 0:NPC] = proj_ref[3]
    up_ref[40:41, 0:NPC] = edge.astype(F32)
    up_ref[41:42, 0:GHOST] = jnp.concatenate(inverse, axis=1)
    up_ref[42:43, 0:LANES] = atoms
    down_ref[16:17, 0:LANES] = atoms


def split_kernel(x_ref, out_ref):
    out_ref[0], out_ref[1] = split2(x_ref[...])


def local_kernel(conn_ref, send_ref, proj_ref, maps_ref, p_ref, pt_ref):
    least = [jnp.full((1, LANES), 4.0 * NPC, F32)] * (NODES // LANES)
    most = [jnp.full((1, LANES), -1.0, F32)] * (NODES // LANES)
    position = row_iota(NPC, LANES).astype(F32)
    node = lane_iota(NPC, LANES).astype(F32)
    for c in range(4):
        names = column(conn_ref[c : c + 1, :].astype(F32))
        place = position + float(c * NPC)
        thirds = jnp.concatenate(split3(padded_projectors(proj_ref[c])), axis=0)
        for k in range(0, NODES // LANES, 2):
            hits = []
            for j in (k, k + 1):
                same = names == node + float(j * LANES)
                least[j] = jnp.minimum(least[j], jnp.min(jnp.where(same, place, 4.0 * NPC), axis=0, keepdims=True))
                most[j] = jnp.maximum(most[j], jnp.max(jnp.where(same, place, -1.0), axis=0, keepdims=True))
                hits.append(jnp.where(same, 1.0, 0.0).astype(BF16))
            parts = dot(thirds, jnp.concatenate(hits, axis=1))
            p_ref[c * SLOT : (c + 1) * SLOT, k * LANES : (k + 2) * LANES] = parts[:SLOT] + parts[SLOT : 2 * SLOT] + parts[2 * SLOT :]
    inner = jnp.concatenate([p_ref[0 : 3 * SLOT, :], jnp.zeros((SLOT, NODES), F32)], axis=0)
    pt_ref[0], pt_ref[1] = split2(inner.T)
    names = column(send_ref[...].astype(F32))
    maps_ref[...] = jnp.zeros_like(maps_ref)
    for k in range(NODES // LANES):
        here = slice(k * LANES, (k + 1) * LANES)
        maps_ref[0:1, here] = least[k].astype(jnp.int32)
        maps_ref[1:2, here] = jnp.where(most[k] > least[k], most[k], -1.0).astype(jnp.int32)
        same = names == node[:GHOST] + float(k * LANES)
        maps_ref[2:3, here] = jnp.max(jnp.where(same, position[:GHOST], -1.0), axis=0, keepdims=True).astype(jnp.int32)


def joined_kernel(up_ref, down_ref, maps_ref, atom_ref, proj_ref, coupling_ref, pn_ref, p_ref, pe_ref, k_ref, index_ref):
    low_atoms, high_atoms = up_ref[42:43, 0:LANES], down_ref[16:17, 0:LANES]
    which = lane_iota(1, LANES) >> 5
    own = jnp.full((1, LANES), -100.0, F32)
    for c in range(4):
        own = jnp.where(which == c, atom_ref[c].astype(F32), own)
    edge_low = jnp.broadcast_to(low_atoms[:, 96:97] - float(ATOM_DEV), (1, LANES))
    edges = jnp.where(which == 0, atom_ref[3].astype(F32), jnp.where(which == 1, edge_low, -200.0))
    from_upper = jnp.where(which < 3, high_atoms + float(ATOM_DEV), -300.0)
    from_lower = jnp.where(which < 3, low_atoms - float(ATOM_DEV), -400.0)
    source = jnp.concatenate([jnp.where(which < 3, own, -500.0), edges, from_upper, from_lower], axis=1)
    inside = (lane_iota(SLOT, 4 * LANES) & (SLOT - 1)) == row_iota(SLOT, 4 * LANES)
    rows = []
    for c in range(5):
        if c < 4:
            same = source == atom_ref[c].astype(F32)
        else:
            same = source == jnp.concatenate([edge_low] * 4, axis=1)
        rows.append(jnp.where(inside & jnp.broadcast_to(same, inside.shape), 1.0, 0.0))
    rows.append(jnp.zeros((3 * SLOT, 4 * LANES), F32))
    k_ref[...] = jnp.concatenate(rows, axis=0).T.astype(BF16)
    low = padded_projectors(up_ref[16 : 16 + NPROJ, 0:NPC])
    stacked = jnp.concatenate([padded_projectors(proj_ref[3]), low, jnp.zeros((2 * SLOT, NPC), F32)], axis=0)
    pe_ref[0], pe_ref[1] = split2(stacked.T)
    index_ref[...] = jnp.zeros_like(index_ref)
    index_ref[0:2, :] = maps_ref[0:2, :]
    sent = maps_ref[2:3, :]
    rows8 = [jnp.broadcast_to(b, (8, LANES)) for b in blocks_of(up_ref[41:42, 0:GHOST])]
    third = pick_row(rows8, sent)
    third = jnp.where(jnp.broadcast_to(sent, third.shape) >= 0, third, -1.0)[0:1].astype(jnp.int32)
    index_ref[2:3, :] = third
    index_ref[3:4, 0:NPC] = up_ref[40:41, 0:NPC].astype(jnp.int32) - NODES
    size = lax.axis_size("fe")
    fe = lax.axis_index("fe")
    below = lax.rem(fe + size - 1, size)
    row = lane_iota(1, coupling_ref.shape[1])
    offset = row - below * ATOM_DEV
    slots = jnp.where((offset >= 0) & (offset < ATOM_DEV), offset, -600)
    offset = row - fe * ATOM_DEV
    slots = jnp.where((offset >= 0) & (offset < ATOM_DEV), offset + ATOM_DEV, slots).astype(F32)
    factors = []
    for c in range(5):
        name = atom_ref[c].astype(F32) if c < 4 else jnp.broadcast_to(edge_low[:, 0:1], slots.shape)
        mine = jnp.where(jnp.broadcast_to(slots == name, coupling_ref.shape), coupling_ref[...], 0.0)
        factors.append(jnp.sum(mine, axis=1, keepdims=True))
        factors.append(jnp.zeros((SLOT - NPROJ, 1), F32))
    spread = jnp.concatenate([pn_ref[...], pick_row(blocks_of(low), third)], axis=0) * jnp.concatenate(factors, axis=0)
    spread = jnp.concatenate([spread, jnp.zeros((3 * SLOT, NODES), F32)], axis=0)
    p_ref[0], p_ref[1] = split2(spread)


def inner_kernel(mode, v_ref, prev_ref, conn_ref, maps_ref, pot_ref, e_ref, base_ref, *result_ref):
    v = v_ref[...]
    for ref in result_ref:
        ref[...] = v
    sources = blocks_of(v)
    cells = [pick_row(sources, conn_ref[c : c + 1, :]) for c in range(3)]
    x_high, x_low = split2(jnp.concatenate(cells, axis=0))
    y = product(x_high, x_low, e_ref[0], e_ref[1])
    blocks = []
    for c in range(3):
        blocks += blocks_of(y[c * BANDS : (c + 1) * BANDS])
    for k in range(NODES // LANES):
        here = slice(k * LANES, (k + 1) * LANES)
        h = pick(blocks, maps_ref[0:1, here]) + pick(blocks, maps_ref[1:2, here]) + pot_ref[:, here] * v[:, here]
        if mode == "first":
            h = (h - CENTER * v[:, here]) * (1.0 / HALF_WIDTH)
        elif mode == "middle":
            h = (h - CENTER * v[:, here]) * (2.0 / HALF_WIDTH) - prev_ref[:, here]
        base_ref[:, here] = h


def is_odd():
    return lax.rem(lax.axis_index("fe"), 2) == 1


def received(paired, one_ref, two_ref):
    if not paired:
        up, down = one_ref, two_ref
        return up[0:BANDS, 0:NPC], up[0:BANDS, NPC:], down[0:BANDS, 0:GHOST], down[0:BANDS, GHOST:]
    odd = is_odd()
    one, two = one_ref[...], two_ref[...]
    up, down = jnp.where(odd, two, one), jnp.where(odd, one[:, GHOST:], two[:, GHOST:])
    return up[:, 0:NPC], up[:, NPC:], down[:, 0:GHOST], down[:, GHOST:]


def outer(paired, ups_ref, downs_ref, one_ref, two_ref, conn_ref, index_ref, e_ref, p_ref, pe_ref, k_ref):
    from_lower, lower_partials, from_upper, upper_partials = received(paired, one_ref, two_ref)
    edge = ups_ref[0:BANDS, 0:NPC] + pick_row(blocks_of(from_upper), conn_ref[3:4, :] - NODES)
    low = from_lower + pick_row(blocks_of(downs_ref[0:BANDS, 0:GHOST]), index_ref[3:4, 0:NPC])
    x_high, x_low = split2(jnp.concatenate([edge, low], axis=0))
    wide = product(x_high, x_low, pe_ref[0], pe_ref[1])
    which = lane_iota(BANDS, LANES) >> 5
    edges = jnp.where(which == 0, wide[:BANDS], jnp.where(which == 1, wide[BANDS:], 0.0))
    partials = jnp.concatenate([ups_ref[0:BANDS, NPC:], edges, upper_partials, lower_partials], axis=1)
    sums = dot(jnp.concatenate(split3(partials), axis=0), k_ref[...])
    w_high, w_low = split2(sums[0:16] + sums[16:32] + sums[32:48])
    nonlocal_part = product(w_high, w_low, p_ref[0], p_ref[1])
    y = product(x_high, x_low, e_ref[0], e_ref[1])
    own, other = blocks_of(y[:BANDS]), blocks_of(y[BANDS:])
    out = []
    for k in range(NODES // LANES):
        here = slice(k * LANES, (k + 1) * LANES)
        total = pick(own, index_ref[0:1, here], 12) + pick(own, index_ref[1:2, here], 12)
        out.append(total + pick(other, index_ref[2:3, here]))
    return jnp.concatenate(out, axis=1) + nonlocal_part


def outer_kernel(paired, factor, base_ref, ups_ref, downs_ref, one_ref, two_ref, conn_ref, index_ref, e_ref, p_ref, pe_ref, k_ref,
                 send_ref, pt_ref, new_ref, upo_ref, downo_ref, oneo_ref, twoo_ref, *copies_ref):
    h = outer(paired, ups_ref, downs_ref, one_ref, two_ref, conn_ref, index_ref, e_ref, p_ref, pe_ref, k_ref)
    new = base_ref[...] + h * factor
    new_ref[...] = new
    for ref in copies_ref:
        for i in range(ref.shape[0]):
            ref[i] = new
    v_high, v_low = split2(new)
    pack_message(new, product(v_high, v_low, pt_ref[0], pt_ref[1]), conn_ref, send_ref, upo_ref, downo_ref)
    up = upo_ref[...]
    down = jnp.concatenate([jnp.zeros((BANDS, GHOST), F32), downo_ref[...]], axis=1)
    odd = is_odd()
    oneo_ref[...] = jnp.where(odd, up, down)
    twoo_ref[...] = jnp.where(odd, down, up)


def gram_kernel(base_ref, ups_ref, downs_ref, one_ref, two_ref, conn_ref, index_ref, e_ref, p_ref, pe_ref, k_ref,
                v_ref, all_ref, out_ref):
    h = base_ref[...] + outer(True, ups_ref, downs_ref, one_ref, two_ref, conn_ref, index_ref, e_ref, p_ref, pe_ref, k_ref)
    s_high, s_low = split2(jnp.concatenate([h, v_ref[...]], axis=0))
    a_high, a_low = split2(all_ref[...])
    both = dot_nt(jnp.concatenate([s_high, s_low], axis=0), a_high)
    panel = both[:32] + both[32:] + dot_nt(s_high, a_low)
    for i in range(out_ref.shape[0]):
        out_ref[i] = panel


def add_kernel(parts_ref, out_ref):
    total = parts_ref[0]
    for i in range(1, parts_ref.shape[0]):
        total = total + parts_ref[i]
    for i in range(out_ref.shape[0]):
        out_ref[i] = total


def last_kernel(scale, parts_ref, projected_ref, correlation_ref):
    total = parts_ref[0]
    for i in range(1, parts_ref.shape[0]):
        total = total + parts_ref[i]
    projected_ref[...] = total[0:BANDS] * scale
    correlation_ref[...] = total[BANDS:] * scale


VM = pl.BlockSpec(memory_space=pltpu.VMEM)
SM = pl.BlockSpec(memory_space=pltpu.SMEM)


def call(kernel, outs, ins, *args):
    return pl.pallas_call(
        kernel,
        out_shape=[jax.ShapeDtypeStruct(s, t) for s, t in outs],
        in_specs=ins,
        out_specs=[VM] * len(outs),
        compiler_params=pltpu.CompilerParams(vmem_limit_bytes=24 * 2**20),
    )(*args)


def shifted(block, distance):
    size = lax.axis_size("fe")
    return lax.ppermute(block, "fe", [(i, (i + distance) % size) for i in range(size)])


def swapped(block, first):
    size = lax.axis_size("fe")
    return lax.ppermute(block, "fe", [(i, (i + 1 if i % 2 == first else i - 1) % size) for i in range(size)])


def on_device(wavefunctions, potential, element_matrix, projectors, coupling, connectivity, send_list, atom_of_cell):
    fe_count = lax.axis_size("fe")
    v, conn, send = wavefunctions, connectivity, send_list.reshape(1, GHOST)
    pot, couple = potential.reshape(1, NODES), coupling.T
    ups, downs = call(
        first_kernel,
        [((48, 640), F32), ((24, 384), F32)],
        [VM, VM, VM, SM, VM, VM, VM],
        v, conn, send, atom_of_cell, projectors, pot, couple,
    )
    up, down = shifted(ups, 1), shifted(downs, -1)
    maps, pn, pt = call(
        local_kernel,
        [((8, NODES), jnp.int32), ((4 * SLOT, NODES), F32), ((2, NODES, LANES), BF16)],
        [VM] * 3,
        conn, send, projectors,
    )
    (e,) = call(split_kernel, [((2, NPC, NPC), BF16)], [VM], element_matrix)

    def inner(mode, v, previous):
        outs = [((BANDS, NODES), F32)] * (2 if mode == "last" else 1)
        return call(functools.partial(inner_kernel, mode), outs, [VM] * 6, v, previous, conn, maps, pot, e)

    previous = current = v
    (base,) = inner("first", current, previous)
    p, pe, k, index = call(
        joined_kernel,
        [((2, 256, NODES), BF16), ((2, NPC, LANES), BF16), ((512, 256), BF16), ((8, NODES), jnp.int32)],
        [VM, VM, VM, SM, VM, VM, VM],
        up, down, maps, atom_of_cell, projectors, couple, pn,
    )
    shared = (conn, index, e, p, pe, k)
    for step in range(DEGREE):
        last = step == DEGREE - 1
        copied = [((lax.axis_size("band"), BANDS, NODES), F32)] if last else []
        new, ups, downs, one, two, *copied = call(
            functools.partial(outer_kernel, step > 0, (1.0 if step == 0 else 2.0) / HALF_WIDTH),
            [((BANDS, NODES), F32), ((BANDS, 640), F32), ((BANDS, 384), F32), ((BANDS, 640), F32), ((BANDS, 640), F32)] + copied,
            [VM] * 13,
            base, ups, downs, up, down, *shared, send, pt,
        )
        previous, current = current, new
        if last:
            everyone = lax.all_to_all(copied[0], "band", 0, 0).reshape(-1, NODES)
        up, down = swapped(one, 1), swapped(two, 0)
        base, *result = inner("last" if last else "middle", current, current if last else previous)
    (copies,) = call(
        gram_kernel,
        [((8, 32, LANES), F32)],
        [VM] * 13,
        base, ups, downs, up, down, *shared, current, everyone,
    )
    near = [[8 * i + j for j in range(8)] for i in range(fe_count // 8)]
    far = [[8 * i + j for i in range(fe_count // 8)] for j in range(8)]
    parts = lax.all_to_all(copies, "fe", 0, 0, axis_index_groups=near)
    (copies,) = call(add_kernel, [((fe_count // 8, 32, LANES), F32)], [VM], parts)
    parts = lax.all_to_all(copies, "fe", 0, 0, axis_index_groups=far)
    projected, correlation = call(
        functools.partial(last_kernel, 1.0 / (NODES * fe_count)),
        [((BANDS, LANES), F32), ((BANDS, LANES), F32)],
        [VM],
        parts,
    )
    return result[0], projected.T, correlation.T


def solution(mesh):
    in_specs = (
        P("band", "fe"),
        P("fe"),
        P(),
        P("fe", None, None),
        P(),
        P("fe", None),
        P("fe"),
        P("fe"),
    )
    out_specs = (P("band", "fe"), P(None, "band"), P(None, "band"))
    return jax.shard_map(on_device, mesh=mesh, in_specs=in_specs, out_specs=out_specs, check_vma=False)
```

```python
import functools

import jax
import jax.numpy as jnp
from jax import lax
from jax.experimental import pallas as pl
from jax.experimental.pallas import tpu as pltpu
from jax.sharding import PartitionSpec as P

NPROJ = 18
ATOM_DEV = 8
DEGREE = 6
CENTER = 0.9
HALF_WIDTH = 1.1
BANDS = 16
NODES = 1024
NPC = 512
GHOST = 256
LANES = 128
SLOT = 32
F32 = jnp.float32
BF16 = jnp.bfloat16


def dot(a, b):
    return lax.dot_general(a, b, (((1,), (0,)), ((), ())), preferred_element_type=F32)


def dot_nt(a, b):
    return lax.dot_general(a, b, (((1,), (1,)), ((), ())), preferred_element_type=F32)


def split2(x):
    high = x.astype(BF16)
    return high, (x - high.astype(F32)).astype(BF16)


def split3(x):
    high = x.astype(BF16)
    rest = x - high.astype(F32)
    mid = rest.astype(BF16)
    return high, mid, (rest - mid.astype(F32)).astype(BF16)


def product(x_high, x_low, w_high, w_low):
    rows = x_high.shape[0]
    less = dot(x_high, w_low)
    both = dot(jnp.concatenate([x_high, x_low], axis=0), w_high)
    return both[:rows] + (both[rows:] + less)


def blocks_of(x):
    return [x[:, i : i + LANES] for i in range(0, x.shape[1], LANES)]


def pick(sources, index, first=0):
    rows = sources[0].shape[0]
    index = jnp.broadcast_to(index, (rows, LANES))
    lane = index & (LANES - 1)
    block = index >> 7
    total = jnp.zeros((rows, LANES), F32)
    for k, source in enumerate(sources):
        value = jnp.take_along_axis(source, lane, axis=1, mode="promise_in_bounds")
        total = jnp.where(block == first + k, value, total)
    return total


def pick_row(sources, index, first=0):
    return jnp.concatenate([pick(sources, i, first) for i in blocks_of(index)], axis=1)


def column(row):
    return jnp.broadcast_to(row, (LANES, row.shape[1])).T


def lane_iota(rows, lanes):
    return lax.broadcasted_iota(jnp.int32, (rows, lanes), 1)


def row_iota(rows, lanes):
    return lax.broadcasted_iota(jnp.int32, (rows, lanes), 0)


def padded_projectors(cell):
    return jnp.concatenate([cell, jnp.zeros((SLOT - NPROJ, NPC), F32)], axis=0)


def pack_message(vectors, partials, conn_ref, send_ref, up_ref, down_ref):
    sources = blocks_of(vectors)
    up_ref[0:BANDS, 0:NPC] = pick_row(sources, conn_ref[3:4, :])
    up_ref[0:BANDS, NPC:] = partials
    down_ref[0:BANDS, 0:GHOST] = pick_row(sources, send_ref[...])
    down_ref[0:BANDS, GHOST:] = partials


def first_kernel(v_ref, conn_ref, send_ref, atom_ref, proj_ref, pot_ref, coupling_ref, up_ref, down_ref):
    v = v_ref[...]
    sources = blocks_of(v)
    cells = [pick_row(sources, conn_ref[c : c + 1, :]) for c in range(3)]
    stacked = [padded_projectors(proj_ref[c]) for c in range(3)] + [jnp.zeros((SLOT, NPC), F32)]
    t_high, t_low = split2(jnp.concatenate(stacked, axis=0).T)
    x_high, x_low = split2(jnp.concatenate(cells, axis=0))
    wide = product(x_high, x_low, t_high, t_low)
    which = lane_iota(BANDS, LANES) >> 5
    partials = jnp.zeros((BANDS, LANES), F32)
    for c in range(3):
        partials = jnp.where(which == c, wide[c * BANDS : (c + 1) * BANDS], partials)
    which = lane_iota(1, LANES) >> 5
    atoms = jnp.zeros((1, LANES), F32)
    for c in range(4):
        atoms = jnp.where(which == c, atom_ref[c].astype(F32), atoms)
    edge = conn_ref[3:4, :]
    names = column(edge.astype(F32))
    position = row_iota(NPC, LANES).astype(F32)
    inverse = []
    for k in range(GHOST // LANES):
        slot = (lane_iota(NPC, LANES) + (NODES + k * LANES)).astype(F32)
        inverse.append(jnp.max(jnp.where(names == slot, position, -1.0), axis=0, keepdims=True))
    up_ref[...] = jnp.zeros_like(up_ref)
    down_ref[...] = jnp.zeros_like(down_ref)
    pack_message(v, partials, conn_ref, send_ref, up_ref, down_ref)
    up_ref[16 : 16 + NPROJ, 0:NPC] = proj_ref[3]
    up_ref[40:41, 0:NPC] = edge.astype(F32)
    up_ref[41:42, 0:GHOST] = jnp.concatenate(inverse, axis=1)
    up_ref[42:43, 0:LANES] = atoms
    down_ref[16:17, 0:LANES] = atoms


def split_kernel(x_ref, out_ref):
    out_ref[0], out_ref[1] = split2(x_ref[...])


def local_kernel(conn_ref, send_ref, proj_ref, maps_ref, p_ref, pt_ref):
    least = [jnp.full((1, LANES), 4.0 * NPC, F32)] * (NODES // LANES)
    most = [jnp.full((1, LANES), -1.0, F32)] * (NODES // LANES)
    position = row_iota(NPC, LANES).astype(F32)
    node = lane_iota(NPC, LANES).astype(F32)
    for c in range(4):
        names = column(conn_ref[c : c + 1, :].astype(F32))
        place = position + float(c * NPC)
        thirds = jnp.concatenate(split3(padded_projectors(proj_ref[c])), axis=0)
        for k in range(0, NODES // LANES, 2):
            hits = []
            for j in (k, k + 1):
                same = names == node + float(j * LANES)
                least[j] = jnp.minimum(least[j], jnp.min(jnp.where(same, place, 4.0 * NPC), axis=0, keepdims=True))
                most[j] = jnp.maximum(most[j], jnp.max(jnp.where(same, place, -1.0), axis=0, keepdims=True))
                hits.append(jnp.where(same, 1.0, 0.0).astype(BF16))
            parts = dot(thirds, jnp.concatenate(hits, axis=1))
            p_ref[c * SLOT : (c + 1) * SLOT, k * LANES : (k + 2) * LANES] = parts[:SLOT] + parts[SLOT : 2 * SLOT] + parts[2 * SLOT :]
    inner = jnp.concatenate([p_ref[0 : 3 * SLOT, :], jnp.zeros((SLOT, NODES), F32)], axis=0)
    pt_ref[0], pt_ref[1] = split2(inner.T)
    names = column(send_ref[...].astype(F32))
    maps_ref[...] = jnp.zeros_like(maps_ref)
    for k in range(NODES // LANES):
        here = slice(k * LANES, (k + 1) * LANES)
        maps_ref[0:1, here] = least[k].astype(jnp.int32)
        maps_ref[1:2, here] = jnp.where(most[k] > least[k], most[k], -1.0).astype(jnp.int32)
        same = names == node[:GHOST] + float(k * LANES)
        maps_ref[2:3, here] = jnp.max(jnp.where(same, position[:GHOST], -1.0), axis=0, keepdims=True).astype(jnp.int32)


def joined_kernel(up_ref, down_ref, maps_ref, atom_ref, proj_ref, coupling_ref, pn_ref, p_ref, pe_ref, k_ref, index_ref):
    low_atoms, high_atoms = up_ref[42:43, 0:LANES], down_ref[16:17, 0:LANES]
    which = lane_iota(1, LANES) >> 5
    own = jnp.full((1, LANES), -100.0, F32)
    for c in range(4):
        own = jnp.where(which == c, atom_ref[c].astype(F32), own)
    edge_low = jnp.broadcast_to(low_atoms[:, 96:97] - float(ATOM_DEV), (1, LANES))
    edges = jnp.where(which == 0, atom_ref[3].astype(F32), jnp.where(which == 1, edge_low, -200.0))
    from_upper = jnp.where(which < 3, high_atoms + float(ATOM_DEV), -300.0)
    from_lower = jnp.where(which < 3, low_atoms - float(ATOM_DEV), -400.0)
    source = jnp.concatenate([jnp.where(which < 3, own, -500.0), edges, from_upper, from_lower], axis=1)
    inside = (lane_iota(SLOT, 4 * LANES) & (SLOT - 1)) == row_iota(SLOT, 4 * LANES)
    rows = []
    for c in range(5):
        if c < 4:
            same = source == atom_ref[c].astype(F32)
        else:
            same = source == jnp.concatenate([edge_low] * 4, axis=1)
        rows.append(jnp.where(inside & jnp.broadcast_to(same, inside.shape), 1.0, 0.0))
    rows.append(jnp.zeros((3 * SLOT, 4 * LANES), F32))
    k_ref[...] = jnp.concatenate(rows, axis=0).T.astype(BF16)
    low = padded_projectors(up_ref[16 : 16 + NPROJ, 0:NPC])
    stacked = jnp.concatenate([padded_projectors(proj_ref[3]), low, jnp.zeros((2 * SLOT, NPC), F32)], axis=0)
    pe_ref[0], pe_ref[1] = split2(stacked.T)
    index_ref[...] = jnp.zeros_like(index_ref)
    index_ref[0:2, :] = maps_ref[0:2, :]
    sent = maps_ref[2:3, :]
    rows8 = [jnp.broadcast_to(b, (8, LANES)) for b in blocks_of(up_ref[41:42, 0:GHOST])]
    third = pick_row(rows8, sent)
    third = jnp.where(jnp.broadcast_to(sent, third.shape) >= 0, third, -1.0)[0:1].astype(jnp.int32)
    index_ref[2:3, :] = third
    index_ref[3:4, 0:NPC] = up_ref[40:41, 0:NPC].astype(jnp.int32) - NODES
    size = lax.axis_size("fe")
    fe = lax.axis_index("fe")
    below = lax.rem(fe + size - 1, size)
    row = lane_iota(1, coupling_ref.shape[1])
    offset = row - below * ATOM_DEV
    slots = jnp.where((offset >= 0) & (offset < ATOM_DEV), offset, -600)
    offset = row - fe * ATOM_DEV
    slots = jnp.where((offset >= 0) & (offset < ATOM_DEV), offset + ATOM_DEV, slots).astype(F32)
    factors = []
    for c in range(5):
        name = atom_ref[c].astype(F32) if c < 4 else jnp.broadcast_to(edge_low[:, 0:1], slots.shape)
        mine = jnp.where(jnp.broadcast_to(slots == name, coupling_ref.shape), coupling_ref[...], 0.0)
        factors.append(jnp.sum(mine, axis=1, keepdims=True))
        factors.append(jnp.zeros((SLOT - NPROJ, 1), F32))
    spread = jnp.concatenate([pn_ref[...], pick_row(blocks_of(low), third)], axis=0) * jnp.concatenate(factors, axis=0)
    spread = jnp.concatenate([spread, jnp.zeros((3 * SLOT, NODES), F32)], axis=0)
    p_ref[0], p_ref[1] = split2(spread)


def inner_kernel(mode, v_ref, prev_ref, conn_ref, maps_ref, pot_ref, e_ref, base_ref, *result_ref):
    v = v_ref[...]
    for ref in result_ref:
        ref[...] = v
    sources = blocks_of(v)
    cells = [pick_row(sources, conn_ref[c : c + 1, :]) for c in range(3)]
    x_high, x_low = split2(jnp.concatenate(cells, axis=0))
    y = product(x_high, x_low, e_ref[0], e_ref[1])
    blocks = []
    for c in range(3):
        blocks += blocks_of(y[c * BANDS : (c + 1) * BANDS])
    for k in range(NODES // LANES):
        here = slice(k * LANES, (k + 1) * LANES)
        h = pick(blocks, maps_ref[0:1, here]) + pick(blocks, maps_ref[1:2, here]) + pot_ref[:, here] * v[:, here]
        if mode == "first":
            h = (h - CENTER * v[:, here]) * (1.0 / HALF_WIDTH)
        elif mode == "middle":
            h = (h - CENTER * v[:, here]) * (2.0 / HALF_WIDTH) - prev_ref[:, here]
        base_ref[:, here] = h


def is_odd():
    return lax.rem(lax.axis_index("fe"), 2) == 1


def received(paired, one_ref, two_ref):
    if not paired:
        up, down = one_ref, two_ref
        return up[0:BANDS, 0:NPC], up[0:BANDS, NPC:], down[0:BANDS, 0:GHOST], down[0:BANDS, GHOST:]
    odd = is_odd()
    one, two = one_ref[...], two_ref[...]
    up, down = jnp.where(odd, two, one), jnp.where(odd, one[:, GHOST:], two[:, GHOST:])
    return up[:, 0:NPC], up[:, NPC:], down[:, 0:GHOST], down[:, GHOST:]


def outer(paired, ups_ref, downs_ref, one_ref, two_ref, conn_ref, index_ref, e_ref, p_ref, pe_ref, k_ref):
    from_lower, lower_partials, from_upper, upper_partials = received(paired, one_ref, two_ref)
    edge = ups_ref[0:BANDS, 0:NPC] + pick_row(blocks_of(from_upper), conn_ref[3:4, :] - NODES)
    low = from_lower + pick_row(blocks_of(downs_ref[0:BANDS, 0:GHOST]), index_ref[3:4, 0:NPC])
    x_high, x_low = split2(jnp.concatenate([edge, low], axis=0))
    y = product(x_high, x_low, e_ref[0], e_ref[1])
    wide = product(x_high, x_low, pe_ref[0], pe_ref[1])
    which = lane_iota(BANDS, LANES) >> 5
    edges = jnp.where(which == 0, wide[:BANDS], jnp.where(which == 1, wide[BANDS:], 0.0))
    partials = jnp.concatenate([ups_ref[0:BANDS, NPC:], edges, upper_partials, lower_partials], axis=1)
    sums = dot(jnp.concatenate(split3(partials), axis=0), k_ref[...])
    w_high, w_low = split2(sums[0:16] + sums[16:32] + sums[32:48])
    nonlocal_part = product(w_high, w_low, p_ref[0], p_ref[1])
    own, other = blocks_of(y[:BANDS]), blocks_of(y[BANDS:])
    out = []
    for k in range(NODES // LANES):
        here = slice(k * LANES, (k + 1) * LANES)
        total = pick(own, index_ref[0:1, here], 12) + pick(own, index_ref[1:2, here], 12)
        out.append(total + pick(other, index_ref[2:3, here]))
    return jnp.concatenate(out, axis=1) + nonlocal_part


def outer_kernel(paired, factor, base_ref, ups_ref, downs_ref, one_ref, two_ref, conn_ref, index_ref, e_ref, p_ref, pe_ref, k_ref,
                 send_ref, pt_ref, new_ref, upo_ref, downo_ref, oneo_ref, twoo_ref, *copies_ref):
    h = outer(paired, ups_ref, downs_ref, one_ref, two_ref, conn_ref, index_ref, e_ref, p_ref, pe_ref, k_ref)
    new = base_ref[...] + h * factor
    new_ref[...] = new
    for ref in copies_ref:
        for i in range(ref.shape[0]):
            ref[i] = new
    v_high, v_low = split2(new)
    pack_message(new, product(v_high, v_low, pt_ref[0], pt_ref[1]), conn_ref, send_ref, upo_ref, downo_ref)
    up = upo_ref[...]
    down = jnp.concatenate([jnp.zeros((BANDS, GHOST), F32), downo_ref[...]], axis=1)
    odd = is_odd()
    oneo_ref[...] = jnp.where(odd, up, down)
    twoo_ref[...] = jnp.where(odd, down, up)


def gram_kernel(base_ref, ups_ref, downs_ref, one_ref, two_ref, conn_ref, index_ref, e_ref, p_ref, pe_ref, k_ref,
                v_ref, all_ref, out_ref):
    a_high, a_low = split2(all_ref[...])

    def against_all(x):
        x_high, x_low = split2(x)
        less = dot_nt(x_high, a_low)
        both = dot_nt(jnp.concatenate([x_high, x_low], axis=0), a_high)
        return both[:BANDS] + (both[BANDS:] + less)

    correlation = against_all(v_ref[...])
    h = base_ref[...] + outer(True, ups_ref, downs_ref, one_ref, two_ref, conn_ref, index_ref, e_ref, p_ref, pe_ref, k_ref)
    panel = jnp.concatenate([against_all(h), correlation], axis=0)
    for i in range(out_ref.shape[0]):
        out_ref[i] = panel


def add_kernel(parts_ref, out_ref):
    total = parts_ref[0]
    for i in range(1, parts_ref.shape[0]):
        total = total + parts_ref[i]
    for i in range(out_ref.shape[0]):
        out_ref[i] = total


def last_kernel(scale, parts_ref, projected_ref, correlation_ref):
    total = parts_ref[0]
    for i in range(1, parts_ref.shape[0]):
        total = total + parts_ref[i]
    projected_ref[...] = total[0:BANDS] * scale
    correlation_ref[...] = total[BANDS:] * scale


VM = pl.BlockSpec(memory_space=pltpu.VMEM)
SM = pl.BlockSpec(memory_space=pltpu.SMEM)


def call(kernel, outs, ins, *args):
    return pl.pallas_call(
        kernel,
        out_shape=[jax.ShapeDtypeStruct(s, t) for s, t in outs],
        in_specs=ins,
        out_specs=[VM] * len(outs),
        compiler_params=pltpu.CompilerParams(vmem_limit_bytes=24 * 2**20),
    )(*args)


def shifted(block, distance):
    size = lax.axis_size("fe")
    return lax.ppermute(block, "fe", [(i, (i + distance) % size) for i in range(size)])


def swapped(block, first):
    size = lax.axis_size("fe")
    return lax.ppermute(block, "fe", [(i, (i + 1 if i % 2 == first else i - 1) % size) for i in range(size)])


def on_device(wavefunctions, potential, element_matrix, projectors, coupling, connectivity, send_list, atom_of_cell):
    fe_count = lax.axis_size("fe")
    v, conn, send = wavefunctions, connectivity, send_list.reshape(1, GHOST)
    pot, couple = potential.reshape(1, NODES), coupling.T
    ups, downs = call(
        first_kernel,
        [((48, 640), F32), ((24, 384), F32)],
        [VM, VM, VM, SM, VM, VM, VM],
        v, conn, send, atom_of_cell, projectors, pot, couple,
    )
    up, down = shifted(ups, 1), shifted(downs, -1)
    maps, pn, pt = call(
        local_kernel,
        [((8, NODES), jnp.int32), ((4 * SLOT, NODES), F32), ((2, NODES, LANES), BF16)],
        [VM] * 3,
        conn, send, projectors,
    )
    (e,) = call(split_kernel, [((2, NPC, NPC), BF16)], [VM], element_matrix)

    def inner(mode, v, previous):
        outs = [((BANDS, NODES), F32)] * (2 if mode == "last" else 1)
        return call(functools.partial(inner_kernel, mode), outs, [VM] * 6, v, previous, conn, maps, pot, e)

    previous = current = v
    (base,) = inner("first", current, previous)
    p, pe, k, index = call(
        joined_kernel,
        [((2, 256, NODES), BF16), ((2, NPC, LANES), BF16), ((512, 256), BF16), ((8, NODES), jnp.int32)],
        [VM, VM, VM, SM, VM, VM, VM],
        up, down, maps, atom_of_cell, projectors, couple, pn,
    )
    shared = (conn, index, e, p, pe, k)
    for step in range(DEGREE):
        last = step == DEGREE - 1
        copied = [((lax.axis_size("band"), BANDS, NODES), F32)] if last else []
        new, ups, downs, one, two, *copied = call(
            functools.partial(outer_kernel, step > 0, (1.0 if step == 0 else 2.0) / HALF_WIDTH),
            [((BANDS, NODES), F32), ((BANDS, 640), F32), ((BANDS, 384), F32), ((BANDS, 640), F32), ((BANDS, 640), F32)] + copied,
            [VM] * 13,
            base, ups, downs, up, down, *shared, send, pt,
        )
        previous, current = current, new
        if last:
            everyone = lax.all_to_all(copied[0], "band", 0, 0).reshape(-1, NODES)
        up, down = swapped(one, 1), swapped(two, 0)
        base, *result = inner("last" if last else "middle", current, current if last else previous)
    (copies,) = call(
        gram_kernel,
        [((8, 32, LANES), F32)],
        [VM] * 13,
        base, ups, downs, up, down, *shared, current, everyone,
    )
    near = [[8 * i + j for j in range(8)] for i in range(fe_count // 8)]
    far = [[8 * i + j for i in range(fe_count // 8)] for j in range(8)]
    parts = lax.all_to_all(copies, "fe", 0, 0, axis_index_groups=near)
    (copies,) = call(add_kernel, [((fe_count // 8, 32, LANES), F32)], [VM], parts)
    parts = lax.all_to_all(copies, "fe", 0, 0, axis_index_groups=far)
    projected, correlation = call(
        functools.partial(last_kernel, 1.0 / (NODES * fe_count)),
        [((BANDS, LANES), F32), ((BANDS, LANES), F32)],
        [VM],
        parts,
    )
    return result[0], projected.T, correlation.T


def solution(mesh):
    in_specs = (
        P("band", "fe"),
        P("fe"),
        P(),
        P("fe", None, None),
        P(),
        P("fe", None),
        P("fe"),
        P("fe"),
    )
    out_specs = (P("band", "fe"), P(None, "band"), P(None, "band"))
    return jax.shard_map(on_device, mesh=mesh, in_specs=in_specs, out_specs=out_specs, check_vma=False)
```

```python
import functools

import jax
import jax.numpy as jnp
from jax import lax
from jax.experimental import pallas as pl
from jax.experimental.pallas import tpu as pltpu
from jax.sharding import PartitionSpec as P

NPROJ = 18
ATOM_DEV = 8
DEGREE = 6
CENTER = 0.9
HALF_WIDTH = 1.1
BANDS = 16
NODES = 1024
NPC = 512
GHOST = 256
LANES = 128
SLOT = 32
F32 = jnp.float32
BF16 = jnp.bfloat16


def dot(a, b):
    return lax.dot_general(a, b, (((1,), (0,)), ((), ())), preferred_element_type=F32)


def dot_nt(a, b):
    return lax.dot_general(a, b, (((1,), (1,)), ((), ())), preferred_element_type=F32)


def split2(x):
    high = x.astype(BF16)
    return high, (x - high.astype(F32)).astype(BF16)


def split3(x):
    high = x.astype(BF16)
    rest = x - high.astype(F32)
    mid = rest.astype(BF16)
    return high, mid, (rest - mid.astype(F32)).astype(BF16)


def product(x_high, x_low, w_high, w_low):
    rows = x_high.shape[0]
    less = dot(x_high, w_low)
    both = dot(jnp.concatenate([x_high, x_low], axis=0), w_high)
    return both[:rows] + (both[rows:] + less)


def blocks_of(x):
    return [x[:, i : i + LANES] for i in range(0, x.shape[1], LANES)]


def pick(sources, index, first=0):
    rows = sources[0].shape[0]
    index = jnp.broadcast_to(index, (rows, LANES))
    lane = index & (LANES - 1)
    block = index >> 7
    total = jnp.zeros((rows, LANES), F32)
    for k, source in enumerate(sources):
        value = jnp.take_along_axis(source, lane, axis=1, mode="promise_in_bounds")
        total = jnp.where(block == first + k, value, total)
    return total


def pick_row(sources, index, first=0):
    return jnp.concatenate([pick(sources, i, first) for i in blocks_of(index)], axis=1)


def column(row):
    return jnp.broadcast_to(row, (LANES, row.shape[1])).T


def lane_iota(rows, lanes):
    return lax.broadcasted_iota(jnp.int32, (rows, lanes), 1)


def row_iota(rows, lanes):
    return lax.broadcasted_iota(jnp.int32, (rows, lanes), 0)


def padded_projectors(cell):
    return jnp.concatenate([cell, jnp.zeros((SLOT - NPROJ, NPC), F32)], axis=0)


def pack_message(vectors, partials, conn_ref, send_ref, up_ref, down_ref):
    sources = blocks_of(vectors)
    up_ref[0:BANDS, 0:NPC] = pick_row(sources, conn_ref[3:4, :])
    up_ref[0:BANDS, NPC:] = partials
    down_ref[0:BANDS, 0:GHOST] = pick_row(sources, send_ref[...])
    down_ref[0:BANDS, GHOST:] = partials


def first_kernel(v_ref, conn_ref, send_ref, atom_ref, proj_ref, pot_ref, coupling_ref, up_ref, down_ref):
    v = v_ref[...]
    sources = blocks_of(v)
    cells = [pick_row(sources, conn_ref[c : c + 1, :]) for c in range(3)]
    stacked = [padded_projectors(proj_ref[c]) for c in range(3)] + [jnp.zeros((SLOT, NPC), F32)]
    t_high, t_low = split2(jnp.concatenate(stacked, axis=0).T)
    x_high, x_low = split2(jnp.concatenate(cells, axis=0))
    wide = product(x_high, x_low, t_high, t_low)
    which = lane_iota(BANDS, LANES) >> 5
    partials = jnp.zeros((BANDS, LANES), F32)
    for c in range(3):
        partials = jnp.where(which == c, wide[c * BANDS : (c + 1) * BANDS], partials)
    which = lane_iota(1, LANES) >> 5
    atoms = jnp.zeros((1, LANES), F32)
    for c in range(4):
        atoms = jnp.where(which == c, atom_ref[c].astype(F32), atoms)
    edge = conn_ref[3:4, :]
    names = column(edge.astype(F32))
    position = row_iota(NPC, LANES).astype(F32)
    inverse = []
    for k in range(GHOST // LANES):
        slot = (lane_iota(NPC, LANES) + (NODES + k * LANES)).astype(F32)
        inverse.append(jnp.max(jnp.where(names == slot, position, -1.0), axis=0, keepdims=True))
    up_ref[...] = jnp.zeros_like(up_ref)
    down_ref[...] = jnp.zeros_like(down_ref)
    pack_message(v, partials, conn_ref, send_ref, up_ref, down_ref)
    up_ref[16 : 16 + NPROJ, 0:NPC] = proj_ref[3]
    up_ref[34:35, 0:NPC] = edge.astype(F32)
    up_ref[35:36, 0:GHOST] = jnp.concatenate(inverse, axis=1)
    up_ref[36:37, 0:LANES] = atoms
    down_ref[16:17, 0:LANES] = atoms


def split_kernel(x_ref, out_ref):
    out_ref[0], out_ref[1] = split2(x_ref[...])


def local_kernel(conn_ref, send_ref, proj_ref, maps_ref, p_ref, pt_ref):
    least = [jnp.full((1, LANES), 4.0 * NPC, F32)] * (NODES // LANES)
    most = [jnp.full((1, LANES), -1.0, F32)] * (NODES // LANES)
    position = row_iota(NPC, LANES).astype(F32)
    node = lane_iota(NPC, LANES).astype(F32)
    for c in range(4):
        names = column(conn_ref[c : c + 1, :].astype(F32))
        place = position + float(c * NPC)
        thirds = jnp.concatenate(split3(padded_projectors(proj_ref[c])), axis=0)
        for k in range(0, NODES // LANES, 2):
            hits = []
            for j in (k, k + 1):
                same = names == node + float(j * LANES)
                least[j] = jnp.minimum(least[j], jnp.min(jnp.where(same, place, 4.0 * NPC), axis=0, keepdims=True))
                most[j] = jnp.maximum(most[j], jnp.max(jnp.where(same, place, -1.0), axis=0, keepdims=True))
                hits.append(jnp.where(same, 1.0, 0.0).astype(BF16))
            parts = dot(thirds, jnp.concatenate(hits, axis=1))
            p_ref[c * SLOT : (c + 1) * SLOT, k * LANES : (k + 2) * LANES] = parts[:SLOT] + parts[SLOT : 2 * SLOT] + parts[2 * SLOT :]
    inner = jnp.concatenate([p_ref[0 : 3 * SLOT, :], jnp.zeros((SLOT, NODES), F32)], axis=0)
    pt_ref[0], pt_ref[1] = split2(inner.T)
    names = column(send_ref[...].astype(F32))
    maps_ref[...] = jnp.zeros_like(maps_ref)
    for k in range(NODES // LANES):
        here = slice(k * LANES, (k + 1) * LANES)
        maps_ref[0:1, here] = least[k].astype(jnp.int32)
        maps_ref[1:2, here] = jnp.where(most[k] > least[k], most[k], -1.0).astype(jnp.int32)
        same = names == node[:GHOST] + float(k * LANES)
        maps_ref[2:3, here] = jnp.max(jnp.where(same, position[:GHOST], -1.0), axis=0, keepdims=True).astype(jnp.int32)


def joined_kernel(up_ref, down_ref, maps_ref, atom_ref, proj_ref, coupling_ref, pn_ref, p_ref, pe_ref, k_ref, index_ref):
    low_atoms, high_atoms = up_ref[36:37, 0:LANES], down_ref[16:17, 0:LANES]
    which = lane_iota(1, LANES) >> 5
    own = jnp.full((1, LANES), -100.0, F32)
    for c in range(4):
        own = jnp.where(which == c, atom_ref[c].astype(F32), own)
    edge_low = jnp.broadcast_to(low_atoms[:, 96:97] - float(ATOM_DEV), (1, LANES))
    edges = jnp.where(which == 0, atom_ref[3].astype(F32), jnp.where(which == 1, edge_low, -200.0))
    from_upper = jnp.where(which < 3, high_atoms + float(ATOM_DEV), -300.0)
    from_lower = jnp.where(which < 3, low_atoms - float(ATOM_DEV), -400.0)
    source = jnp.concatenate([jnp.where(which < 3, own, -500.0), edges, from_upper, from_lower], axis=1)
    target = [own, jnp.where(which == 0, edge_low, -700.0)]
    names = column(source)
    inside = (lane_iota(4 * LANES, LANES) & (SLOT - 1)) == (row_iota(4 * LANES, LANES) & (SLOT - 1))
    for i in range(2):
        k_ref[:, i * LANES : (i + 1) * LANES] = jnp.where(inside & (names == target[i]), 1.0, 0.0).astype(BF16)
    low = padded_projectors(up_ref[16 : 16 + NPROJ, 0:NPC])
    stacked = jnp.concatenate([padded_projectors(proj_ref[3]), low, jnp.zeros((2 * SLOT, NPC), F32)], axis=0)
    pe_ref[0], pe_ref[1] = split2(stacked.T)
    index_ref[...] = jnp.zeros_like(index_ref)
    index_ref[0:2, :] = maps_ref[0:2, :]
    sent = maps_ref[2:3, :]
    rows8 = [jnp.broadcast_to(b, (8, LANES)) for b in blocks_of(up_ref[35:36, 0:GHOST])]
    third = pick_row(rows8, sent)
    third = jnp.where(jnp.broadcast_to(sent, third.shape) >= 0, third, -1.0)[0:1].astype(jnp.int32)
    index_ref[2:3, :] = third
    index_ref[3:4, 0:NPC] = up_ref[34:35, 0:NPC].astype(jnp.int32) - NODES
    size = lax.axis_size("fe")
    fe = lax.axis_index("fe")
    below = lax.rem(fe + size - 1, size)
    row = lane_iota(1, coupling_ref.shape[1])
    offset = row - below * ATOM_DEV
    slots = jnp.where((offset >= 0) & (offset < ATOM_DEV), offset, -600)
    offset = row - fe * ATOM_DEV
    slots = jnp.where((offset >= 0) & (offset < ATOM_DEV), offset + ATOM_DEV, slots).astype(F32)
    factors = []
    for c in range(5):
        name = atom_ref[c].astype(F32) if c < 4 else jnp.broadcast_to(edge_low[:, 0:1], slots.shape)
        mine = jnp.where(jnp.broadcast_to(slots == name, coupling_ref.shape), coupling_ref[...], 0.0)
        factors.append(jnp.sum(mine, axis=1, keepdims=True))
        factors.append(jnp.zeros((SLOT - NPROJ, 1), F32))
    spread = jnp.concatenate([pn_ref[...], pick_row(blocks_of(low), third)], axis=0) * jnp.concatenate(factors, axis=0)
    spread = jnp.concatenate([spread, jnp.zeros((3 * SLOT, NODES), F32)], axis=0)
    p_ref[0], p_ref[1] = split2(spread)


def inner_kernel(mode, v_ref, prev_ref, conn_ref, maps_ref, pot_ref, e_ref, base_ref, *result_ref):
    v = v_ref[...]
    for ref in result_ref:
        ref[...] = v
    sources = blocks_of(v)
    cells = [pick_row(sources, conn_ref[c : c + 1, :]) for c in range(3)]
    x_high, x_low = split2(jnp.concatenate(cells, axis=0))
    y = product(x_high, x_low, e_ref[0], e_ref[1])
    blocks = []
    for c in range(3):
        blocks += blocks_of(y[c * BANDS : (c + 1) * BANDS])
    for k in range(NODES // LANES):
        here = slice(k * LANES, (k + 1) * LANES)
        h = pick(blocks, maps_ref[0:1, here]) + pick(blocks, maps_ref[1:2, here]) + pot_ref[:, here] * v[:, here]
        if mode == "first":
            h = (h - CENTER * v[:, here]) * (1.0 / HALF_WIDTH)
        elif mode == "middle":
            h = (h - CENTER * v[:, here]) * (2.0 / HALF_WIDTH) - prev_ref[:, here]
        base_ref[:, here] = h


def is_odd():
    return lax.rem(lax.axis_index("fe"), 2) == 1


def received(paired, one_ref, two_ref):
    if not paired:
        up, down = one_ref, two_ref
        return up[0:BANDS, 0:NPC], up[0:BANDS, NPC:], down[0:BANDS, 0:GHOST], down[0:BANDS, GHOST:]
    odd = is_odd()
    one, two = one_ref[...], two_ref[...]
    up, down = jnp.where(odd, two, one), jnp.where(odd, one[:, GHOST:], two[:, GHOST:])
    return up[:, 0:NPC], up[:, NPC:], down[:, 0:GHOST], down[:, GHOST:]


def outer(paired, ups_ref, downs_ref, one_ref, two_ref, conn_ref, index_ref, e_ref, p_ref, pe_ref, k_ref):
    from_lower, lower_partials, from_upper, upper_partials = received(paired, one_ref, two_ref)
    edge = ups_ref[0:BANDS, 0:NPC] + pick_row(blocks_of(from_upper), conn_ref[3:4, :] - NODES)
    low = from_lower + pick_row(blocks_of(downs_ref[0:BANDS, 0:GHOST]), index_ref[3:4, 0:NPC])
    x_high, x_low = split2(jnp.concatenate([edge, low], axis=0))
    y = product(x_high, x_low, e_ref[0], e_ref[1])
    wide = product(x_high, x_low, pe_ref[0], pe_ref[1])
    which = lane_iota(BANDS, LANES) >> 5
    edges = jnp.where(which == 0, wide[:BANDS], jnp.where(which == 1, wide[BANDS:], 0.0))
    partials = jnp.concatenate([ups_ref[0:BANDS, NPC:], edges, upper_partials, lower_partials], axis=1)
    sums = dot(jnp.concatenate(split3(partials), axis=0), k_ref[...])
    w_high, w_low = split2(sums[0:16] + sums[16:32] + sums[32:48])
    nonlocal_part = product(w_high, w_low, p_ref[0], p_ref[1])
    own, other = blocks_of(y[:BANDS]), blocks_of(y[BANDS:])
    out = []
    for k in range(NODES // LANES):
        here = slice(k * LANES, (k + 1) * LANES)
        total = pick(own, index_ref[0:1, here], 12) + pick(own, index_ref[1:2, here], 12)
        out.append(total + pick(other, index_ref[2:3, here]))
    return jnp.concatenate(out, axis=1) + nonlocal_part


def outer_kernel(paired, factor, base_ref, ups_ref, downs_ref, one_ref, two_ref, conn_ref, index_ref, e_ref, p_ref, pe_ref, k_ref,
                 *rest):
    if len(rest) == 2:
        new_ref, outs = rest[0], rest[1:]
    else:
        new_ref, outs = rest[2], rest[:2] + rest[3:]
    h = outer(paired, ups_ref, downs_ref, one_ref, two_ref, conn_ref, index_ref, e_ref, p_ref, pe_ref, k_ref)
    new = base_ref[...] + h * factor
    new_ref[...] = new
    if len(outs) == 1:
        for i in range(outs[0].shape[0]):
            outs[0][i] = new
    else:
        pack(new, conn_ref, *outs)


def pack(new, conn_ref, send_ref, pt_ref, upo_ref, downo_ref, oneo_ref, twoo_ref):
    v_high, v_low = split2(new)
    pack_message(new, product(v_high, v_low, pt_ref[0], pt_ref[1]), conn_ref, send_ref, upo_ref, downo_ref)
    up = upo_ref[...]
    down = jnp.concatenate([jnp.zeros((BANDS, GHOST), F32), downo_ref[...]], axis=1)
    odd = is_odd()
    oneo_ref[...] = jnp.where(odd, up, down)
    twoo_ref[...] = jnp.where(odd, down, up)


def pack_kernel(new_ref, conn_ref, send_ref, pt_ref, *outs):
    pack(new_ref[...], conn_ref, send_ref, pt_ref, *outs)


def gram_kernel(base_ref, ups_ref, downs_ref, one_ref, two_ref, conn_ref, index_ref, e_ref, p_ref, pe_ref, k_ref,
                v_ref, all_ref, out_ref):
    a_high, a_low = split2(all_ref[...])

    def against_all(x):
        x_high, x_low = split2(x)
        less = dot_nt(x_high, a_low)
        both = dot_nt(jnp.concatenate([x_high, x_low], axis=0), a_high)
        return both[:BANDS] + (both[BANDS:] + less)

    correlation = against_all(v_ref[...])
    h = base_ref[...] + outer(True, ups_ref, downs_ref, one_ref, two_ref, conn_ref, index_ref, e_ref, p_ref, pe_ref, k_ref)
    panel = jnp.concatenate([against_all(h), correlation], axis=0)
    for i in range(out_ref.shape[0]):
        out_ref[i] = panel


def add_kernel(parts_ref, out_ref):
    total = parts_ref[0]
    for i in range(1, parts_ref.shape[0]):
        total = total + parts_ref[i]
    for i in range(out_ref.shape[0]):
        out_ref[i] = total


def last_kernel(scale, parts_ref, projected_ref, correlation_ref):
    total = parts_ref[0]
    for i in range(1, parts_ref.shape[0]):
        total = total + parts_ref[i]
    projected_ref[...] = total[0:BANDS] * scale
    correlation_ref[...] = total[BANDS:] * scale


VM = pl.BlockSpec(memory_space=pltpu.VMEM)
SM = pl.BlockSpec(memory_space=pltpu.SMEM)


def call(kernel, outs, ins, *args):
    return pl.pallas_call(
        kernel,
        out_shape=[jax.ShapeDtypeStruct(s, t) for s, t in outs],
        in_specs=ins,
        out_specs=[VM] * len(outs),
        compiler_params=pltpu.CompilerParams(vmem_limit_bytes=24 * 2**20),
    )(*args)


def shifted(block, distance):
    size = lax.axis_size("fe")
    return lax.ppermute(block, "fe", [(i, (i + distance) % size) for i in range(size)])


def swapped(block, first):
    size = lax.axis_size("fe")
    return lax.ppermute(block, "fe", [(i, (i + 1 if i % 2 == first else i - 1) % size) for i in range(size)])


def on_device(wavefunctions, potential, element_matrix, projectors, coupling, connectivity, send_list, atom_of_cell):
    fe_count = lax.axis_size("fe")
    v, conn, send = wavefunctions, connectivity, send_list.reshape(1, GHOST)
    pot, couple = potential.reshape(1, NODES), coupling.T
    ups, downs = call(
        first_kernel,
        [((40, 640), F32), ((24, 384), F32)],
        [VM, VM, VM, SM, VM, VM, VM],
        v, conn, send, atom_of_cell, projectors, pot, couple,
    )
    up, down = shifted(ups, 1), shifted(downs, -1)
    maps, pn, pt = call(
        local_kernel,
        [((8, NODES), jnp.int32), ((4 * SLOT, NODES), F32), ((2, NODES, LANES), BF16)],
        [VM] * 3,
        conn, send, projectors,
    )
    (e,) = call(split_kernel, [((2, NPC, NPC), BF16)], [VM], element_matrix)

    def inner(mode, v, previous):
        outs = [((BANDS, NODES), F32)] * (2 if mode == "last" else 1)
        return call(functools.partial(inner_kernel, mode), outs, [VM] * 6, v, previous, conn, maps, pot, e)

    previous = current = v
    (base,) = inner("first", current, previous)
    p, pe, k, index = call(
        joined_kernel,
        [((2, 256, NODES), BF16), ((2, NPC, LANES), BF16), ((512, 256), BF16), ((8, NODES), jnp.int32)],
        [VM, VM, VM, SM, VM, VM, VM],
        up, down, maps, atom_of_cell, projectors, couple, pn,
    )
    shared = (conn, index, e, p, pe, k)
    messages = [((BANDS, 640), F32), ((BANDS, 384), F32), ((BANDS, 640), F32), ((BANDS, 640), F32)]
    for step in range(DEGREE):
        last = step == DEGREE - 1
        kernel = functools.partial(outer_kernel, step > 0, (1.0 if step == 0 else 2.0) / HALF_WIDTH)
        vectors = ((BANDS, NODES), F32)
        given = (base, ups, downs, up, down, *shared)
        if last:
            copied = ((lax.axis_size("band"), BANDS, NODES), F32)
            new, copied = call(kernel, [vectors, copied], [VM] * 11, *given)
            everyone = lax.all_to_all(copied, "band", 0, 0).reshape(-1, NODES)
            ups, downs, one, two = call(pack_kernel, messages, [VM] * 4, new, conn, send, pt)
        else:
            new, ups, downs, one, two = call(kernel, [vectors] + messages, [VM] * 13, *given, send, pt)
        previous, current = current, new
        up, down = swapped(one, 1), swapped(two, 0)
        base, *result = inner("last" if last else "middle", current, current if last else previous)
    (copies,) = call(
        gram_kernel,
        [((8, 32, LANES), F32)],
        [VM] * 13,
        base, ups, downs, up, down, *shared, current, everyone,
    )
    near = [[8 * i + j for j in range(8)] for i in range(fe_count // 8)]
    far = [[8 * i + j for i in range(fe_count // 8)] for j in range(8)]
    parts = lax.all_to_all(copies, "fe", 0, 0, axis_index_groups=near)
    (copies,) = call(add_kernel, [((fe_count // 8, 32, LANES), F32)], [VM], parts)
    parts = lax.all_to_all(copies, "fe", 0, 0, axis_index_groups=far)
    projected, correlation = call(
        functools.partial(last_kernel, 1.0 / (NODES * fe_count)),
        [((BANDS, LANES), F32), ((BANDS, LANES), F32)],
        [VM],
        parts,
    )
    return result[0], projected.T, correlation.T


def solution(mesh):
    in_specs = (
        P("band", "fe"),
        P("fe"),
        P(),
        P("fe", None, None),
        P(),
        P("fe", None),
        P("fe"),
        P("fe"),
    )
    out_specs = (P("band", "fe"), P(None, "band"), P(None, "band"))
    return jax.shard_map(on_device, mesh=mesh, in_specs=in_specs, out_specs=out_specs, check_vma=False)
```

```python
import functools

import jax
import jax.numpy as jnp
from jax import lax
from jax.experimental import pallas as pl
from jax.experimental.pallas import tpu as pltpu
from jax.sharding import PartitionSpec as P

NPROJ = 18
ATOM_DEV = 8
DEGREE = 6
CENTER = 0.9
HALF_WIDTH = 1.1
BANDS = 16
NODES = 1024
NPC = 512
GHOST = 256
LANES = 128
SLOT = 32
F32 = jnp.float32
BF16 = jnp.bfloat16


def dot(a, b):
    return lax.dot_general(a, b, (((1,), (0,)), ((), ())), preferred_element_type=F32)


def dot_nt(a, b):
    return lax.dot_general(a, b, (((1,), (1,)), ((), ())), preferred_element_type=F32)


def split2(x):
    high = x.astype(BF16)
    return high, (x - high.astype(F32)).astype(BF16)


def split3(x):
    high = x.astype(BF16)
    rest = x - high.astype(F32)
    mid = rest.astype(BF16)
    return high, mid, (rest - mid.astype(F32)).astype(BF16)


def product(x_high, x_low, w_high, w_low):
    rows = x_high.shape[0]
    less = dot(x_high, w_low)
    both = dot(jnp.concatenate([x_high, x_low], axis=0), w_high)
    return both[:rows] + (both[rows:] + less)


def blocks_of(x):
    return [x[:, i : i + LANES] for i in range(0, x.shape[1], LANES)]


def pick(sources, index, first=0):
    rows = sources[0].shape[0]
    index = jnp.broadcast_to(index, (rows, LANES))
    lane = index & (LANES - 1)
    block = index >> 7
    total = jnp.zeros((rows, LANES), F32)
    for k, source in enumerate(sources):
        value = jnp.take_along_axis(source, lane, axis=1, mode="promise_in_bounds")
        total = jnp.where(block == first + k, value, total)
    return total


def pick_row(sources, index, first=0):
    return jnp.concatenate([pick(sources, i, first) for i in blocks_of(index)], axis=1)


def column(row):
    return jnp.broadcast_to(row, (LANES, row.shape[1])).T


def lane_iota(rows, lanes):
    return lax.broadcasted_iota(jnp.int32, (rows, lanes), 1)


def row_iota(rows, lanes):
    return lax.broadcasted_iota(jnp.int32, (rows, lanes), 0)


def padded_projectors(cell):
    return jnp.concatenate([cell, jnp.zeros((SLOT - NPROJ, NPC), F32)], axis=0)


def pack_message(vectors, partials, conn_ref, send_ref, up_ref, down_ref):
    sources = blocks_of(vectors)
    up_ref[0:BANDS, 0:NPC] = pick_row(sources, conn_ref[3:4, :])
    up_ref[0:BANDS, NPC:] = partials
    down_ref[0:BANDS, 0:GHOST] = pick_row(sources, send_ref[...])
    down_ref[0:BANDS, GHOST:] = partials


def first_kernel(v_ref, conn_ref, send_ref, atom_ref, proj_ref, pot_ref, coupling_ref, up_ref, down_ref):
    v = v_ref[...]
    sources = blocks_of(v)
    cells = [pick_row(sources, conn_ref[c : c + 1, :]) for c in range(3)]
    stacked = [padded_projectors(proj_ref[c]) for c in range(3)] + [jnp.zeros((SLOT, NPC), F32)]
    t_high, t_low = split2(jnp.concatenate(stacked, axis=0).T)
    x_high, x_low = split2(jnp.concatenate(cells, axis=0))
    wide = product(x_high, x_low, t_high, t_low)
    which = lane_iota(BANDS, LANES) >> 5
    partials = jnp.zeros((BANDS, LANES), F32)
    for c in range(3):
        partials = jnp.where(which == c, wide[c * BANDS : (c + 1) * BANDS], partials)
    which = lane_iota(1, LANES) >> 5
    atoms = jnp.zeros((1, LANES), F32)
    for c in range(4):
        atoms = jnp.where(which == c, atom_ref[c].astype(F32), atoms)
    edge = conn_ref[3:4, :]
    names = column(edge.astype(F32))
    position = row_iota(NPC, LANES).astype(F32)
    inverse = []
    for k in range(GHOST // LANES):
        slot = (lane_iota(NPC, LANES) + (NODES + k * LANES)).astype(F32)
        inverse.append(jnp.max(jnp.where(names == slot, position, -1.0), axis=0, keepdims=True))
    up_ref[...] = jnp.zeros_like(up_ref)
    down_ref[...] = jnp.zeros_like(down_ref)
    pack_message(v, partials, conn_ref, send_ref, up_ref, down_ref)
    up_ref[16 : 16 + NPROJ, 0:NPC] = proj_ref[3]
    up_ref[34:35, 0:NPC] = edge.astype(F32)
    up_ref[35:36, 0:GHOST] = jnp.concatenate(inverse, axis=1)
    up_ref[36:37, 0:LANES] = atoms
    down_ref[16:17, 0:LANES] = atoms


def split_kernel(x_ref, out_ref):
    out_ref[0], out_ref[1] = split2(x_ref[...])


def local_kernel(conn_ref, send_ref, proj_ref, maps_ref, p_ref, pt_ref):
    least = [jnp.full((1, LANES), 4.0 * NPC, F32)] * (NODES // LANES)
    most = [jnp.full((1, LANES), -1.0, F32)] * (NODES // LANES)
    position = row_iota(NPC, LANES).astype(F32)
    node = lane_iota(NPC, LANES).astype(F32)
    for c in range(4):
        names = column(conn_ref[c : c + 1, :].astype(F32))
        place = position + float(c * NPC)
        thirds = jnp.concatenate(split3(padded_projectors(proj_ref[c])), axis=0)
        for k in range(0, NODES // LANES, 2):
            hits = []
            for j in (k, k + 1):
                same = names == node + float(j * LANES)
                least[j] = jnp.minimum(least[j], jnp.min(jnp.where(same, place, 4.0 * NPC), axis=0, keepdims=True))
                most[j] = jnp.maximum(most[j], jnp.max(jnp.where(same, place, -1.0), axis=0, keepdims=True))
                hits.append(jnp.where(same, 1.0, 0.0).astype(BF16))
            parts = dot(thirds, jnp.concatenate(hits, axis=1))
            p_ref[c * SLOT : (c + 1) * SLOT, k * LANES : (k + 2) * LANES] = parts[:SLOT] + parts[SLOT : 2 * SLOT] + parts[2 * SLOT :]
    inner = jnp.concatenate([p_ref[0 : 3 * SLOT, :], jnp.zeros((SLOT, NODES), F32)], axis=0)
    pt_ref[0], pt_ref[1] = split2(inner.T)
    names = column(send_ref[...].astype(F32))
    maps_ref[...] = jnp.zeros_like(maps_ref)
    for k in range(NODES // LANES):
        here = slice(k * LANES, (k + 1) * LANES)
        maps_ref[0:1, here] = least[k].astype(jnp.int32)
        maps_ref[1:2, here] = jnp.where(most[k] > least[k], most[k], -1.0).astype(jnp.int32)
        same = names == node[:GHOST] + float(k * LANES)
        maps_ref[2:3, here] = jnp.max(jnp.where(same, position[:GHOST], -1.0), axis=0, keepdims=True).astype(jnp.int32)


def joined_kernel(up_ref, down_ref, maps_ref, atom_ref, proj_ref, coupling_ref, pn_ref, p_ref, pe_ref, k_ref, index_ref):
    low_atoms, high_atoms = up_ref[36:37, 0:LANES], down_ref[16:17, 0:LANES]
    which = lane_iota(1, LANES) >> 5
    own = jnp.full((1, LANES), -100.0, F32)
    for c in range(4):
        own = jnp.where(which == c, atom_ref[c].astype(F32), own)
    edge_low = jnp.broadcast_to(low_atoms[:, 96:97] - float(ATOM_DEV), (1, LANES))
    edges = jnp.where(which == 0, atom_ref[3].astype(F32), jnp.where(which == 1, edge_low, -200.0))
    from_upper = jnp.where(which < 3, high_atoms + float(ATOM_DEV), -300.0)
    from_lower = jnp.where(which < 3, low_atoms - float(ATOM_DEV), -400.0)
    source = jnp.concatenate([jnp.where(which < 3, own, -500.0), edges, from_upper, from_lower], axis=1)
    target = [own, jnp.where(which == 0, edge_low, -700.0)]
    names = column(source)
    inside = (lane_iota(4 * LANES, LANES) & (SLOT - 1)) == (row_iota(4 * LANES, LANES) & (SLOT - 1))
    for i in range(2):
        k_ref[:, i * LANES : (i + 1) * LANES] = jnp.where(inside & (names == target[i]), 1.0, 0.0).astype(BF16)
    low = padded_projectors(up_ref[16 : 16 + NPROJ, 0:NPC])
    stacked = jnp.concatenate([padded_projectors(proj_ref[3]), low, jnp.zeros((2 * SLOT, NPC), F32)], axis=0)
    pe_ref[0], pe_ref[1] = split2(stacked.T)
    index_ref[...] = jnp.zeros_like(index_ref)
    index_ref[0:2, :] = maps_ref[0:2, :]
    sent = maps_ref[2:3, :]
    rows8 = [jnp.broadcast_to(b, (8, LANES)) for b in blocks_of(up_ref[35:36, 0:GHOST])]
    third = pick_row(rows8, sent)
    third = jnp.where(jnp.broadcast_to(sent, third.shape) >= 0, third, -1.0)[0:1].astype(jnp.int32)
    index_ref[2:3, :] = third
    index_ref[3:4, 0:NPC] = up_ref[34:35, 0:NPC].astype(jnp.int32) - NODES
    size = lax.axis_size("fe")
    fe = lax.axis_index("fe")
    below = lax.rem(fe + size - 1, size)
    row = lane_iota(1, coupling_ref.shape[1])
    offset = row - below * ATOM_DEV
    slots = jnp.where((offset >= 0) & (offset < ATOM_DEV), offset, -600)
    offset = row - fe * ATOM_DEV
    slots = jnp.where((offset >= 0) & (offset < ATOM_DEV), offset + ATOM_DEV, slots).astype(F32)
    factors = []
    for c in range(5):
        name = atom_ref[c].astype(F32) if c < 4 else jnp.broadcast_to(edge_low[:, 0:1], slots.shape)
        mine = jnp.where(jnp.broadcast_to(slots == name, coupling_ref.shape), coupling_ref[...], 0.0)
        factors.append(jnp.sum(mine, axis=1, keepdims=True))
        factors.append(jnp.zeros((SLOT - NPROJ, 1), F32))
    spread = jnp.concatenate([pn_ref[...], pick_row(blocks_of(low), third)], axis=0) * jnp.concatenate(factors, axis=0)
    spread = jnp.concatenate([spread, jnp.zeros((3 * SLOT, NODES), F32)], axis=0)
    p_ref[0], p_ref[1] = split2(spread)


def inner_kernel(mode, v_ref, prev_ref, conn_ref, maps_ref, pot_ref, e_ref, base_ref, *result_ref):
    v = v_ref[...]
    for ref in result_ref:
        ref[...] = v
    sources = blocks_of(v)
    cells = [pick_row(sources, conn_ref[c : c + 1, :]) for c in range(3)]
    x_high, x_low = split2(jnp.concatenate(cells, axis=0))
    y = product(x_high, x_low, e_ref[0], e_ref[1])
    blocks = []
    for c in range(3):
        blocks += blocks_of(y[c * BANDS : (c + 1) * BANDS])
    for k in range(NODES // LANES):
        here = slice(k * LANES, (k + 1) * LANES)
        h = pick(blocks, maps_ref[0:1, here]) + pick(blocks, maps_ref[1:2, here]) + pot_ref[:, here] * v[:, here]
        if mode == "first":
            h = (h - CENTER * v[:, here]) * (1.0 / HALF_WIDTH)
        elif mode == "middle":
            h = (h - CENTER * v[:, here]) * (2.0 / HALF_WIDTH) - prev_ref[:, here]
        base_ref[:, here] = h


def is_odd():
    return lax.rem(lax.axis_index("fe"), 2) == 1


def received(paired, one_ref, two_ref):
    if not paired:
        up, down = one_ref, two_ref
        return up[0:BANDS, 0:NPC], up[0:BANDS, NPC:], down[0:BANDS, 0:GHOST], down[0:BANDS, GHOST:]
    odd = is_odd()
    one, two = one_ref[...], two_ref[...]
    up, down = jnp.where(odd, two, one), jnp.where(odd, one[:, GHOST:], two[:, GHOST:])
    return up[:, 0:NPC], up[:, NPC:], down[:, 0:GHOST], down[:, GHOST:]


def outer(paired, ups_ref, downs_ref, one_ref, two_ref, conn_ref, index_ref, e_ref, p_ref, pe_ref, k_ref):
    from_lower, lower_partials, from_upper, upper_partials = received(paired, one_ref, two_ref)
    edge = ups_ref[0:BANDS, 0:NPC] + pick_row(blocks_of(from_upper), conn_ref[3:4, :] - NODES)
    low = from_lower + pick_row(blocks_of(downs_ref[0:BANDS, 0:GHOST]), index_ref[3:4, 0:NPC])
    x_high, x_low = split2(jnp.concatenate([edge, low], axis=0))
    y = product(x_high, x_low, e_ref[0], e_ref[1])
    wide = product(x_high, x_low, pe_ref[0], pe_ref[1])
    which = lane_iota(BANDS, LANES) >> 5
    edges = jnp.where(which == 0, wide[:BANDS], jnp.where(which == 1, wide[BANDS:], 0.0))
    partials = jnp.concatenate([ups_ref[0:BANDS, NPC:], edges, upper_partials, lower_partials], axis=1)
    sums = dot(jnp.concatenate(split3(partials), axis=0), k_ref[...])
    w_high, w_low = split2(sums[0:16] + sums[16:32] + sums[32:48])
    nonlocal_part = product(w_high, w_low, p_ref[0], p_ref[1])
    own, other = blocks_of(y[:BANDS]), blocks_of(y[BANDS:])
    out = []
    for k in range(NODES // LANES):
        here = slice(k * LANES, (k + 1) * LANES)
        total = pick(own, index_ref[0:1, here], 12) + pick(own, index_ref[1:2, here], 12)
        out.append(total + pick(other, index_ref[2:3, here]))
    return jnp.concatenate(out, axis=1) + nonlocal_part


def outer_kernel(paired, factor, base_ref, ups_ref, downs_ref, one_ref, two_ref, conn_ref, index_ref, e_ref, p_ref, pe_ref, k_ref,
                 *rest):
    if len(rest) == 2:
        new_ref, outs = rest[0], rest[1:]
    else:
        new_ref, outs = rest[2], rest[:2] + rest[3:]
    h = outer(paired, ups_ref, downs_ref, one_ref, two_ref, conn_ref, index_ref, e_ref, p_ref, pe_ref, k_ref)
    new = base_ref[...] + h * factor
    new_ref[...] = new
    if len(outs) == 1:
        for i in range(outs[0].shape[0]):
            outs[0][i] = new
    else:
        pack(new, conn_ref, *outs)


def pack(new, conn_ref, send_ref, pt_ref, upo_ref, downo_ref, oneo_ref, twoo_ref):
    v_high, v_low = split2(new)
    pack_message(new, product(v_high, v_low, pt_ref[0], pt_ref[1]), conn_ref, send_ref, upo_ref, downo_ref)
    up = upo_ref[...]
    down = jnp.concatenate([jnp.zeros((BANDS, GHOST), F32), downo_ref[...]], axis=1)
    odd = is_odd()
    oneo_ref[...] = jnp.where(odd, up, down)
    twoo_ref[...] = jnp.where(odd, down, up)


def pack_kernel(new_ref, conn_ref, send_ref, pt_ref, *outs):
    pack(new_ref[...], conn_ref, send_ref, pt_ref, *outs)


def gram_kernel(base_ref, ups_ref, downs_ref, one_ref, two_ref, conn_ref, index_ref, e_ref, p_ref, pe_ref, k_ref,
                v_ref, all_in, out_ref, all_ref, sem):
    copy = pltpu.make_async_copy(all_in, all_ref, sem)
    copy.start()
    h = base_ref[...] + outer(True, ups_ref, downs_ref, one_ref, two_ref, conn_ref, index_ref, e_ref, p_ref, pe_ref, k_ref)
    x_high, x_low = split2(jnp.concatenate([h, v_ref[...]], axis=0))
    copy.wait()
    a_high, a_low = split2(all_ref[...])
    less = dot_nt(x_high, a_low)
    both = dot_nt(jnp.concatenate([x_high, x_low], axis=0), a_high)
    panel = both[: 2 * BANDS] + (both[2 * BANDS :] + less)
    for i in range(out_ref.shape[0]):
        out_ref[i] = panel


def add_kernel(parts_ref, out_ref):
    total = parts_ref[0]
    for i in range(1, parts_ref.shape[0]):
        total = total + parts_ref[i]
    for i in range(out_ref.shape[0]):
        out_ref[i] = total


def last_kernel(scale, parts_ref, projected_ref, correlation_ref):
    total = parts_ref[0]
    for i in range(1, parts_ref.shape[0]):
        total = total + parts_ref[i]
    projected_ref[...] = total[0:BANDS] * scale
    correlation_ref[...] = total[BANDS:] * scale


VM = pl.BlockSpec(memory_space=pltpu.VMEM)
SM = pl.BlockSpec(memory_space=pltpu.SMEM)


def call(kernel, outs, ins, *args, scratch=()):
    return pl.pallas_call(
        kernel,
        scratch_shapes=scratch,
        out_shape=[jax.ShapeDtypeStruct(s, t) for s, t in outs],
        in_specs=ins,
        out_specs=[VM] * len(outs),
        compiler_params=pltpu.CompilerParams(vmem_limit_bytes=24 * 2**20),
    )(*args)


def shifted(block, distance):
    size = lax.axis_size("fe")
    return lax.ppermute(block, "fe", [(i, (i + distance) % size) for i in range(size)])


def swapped(block, first):
    size = lax.axis_size("fe")
    return lax.ppermute(block, "fe", [(i, (i + 1 if i % 2 == first else i - 1) % size) for i in range(size)])


def on_device(wavefunctions, potential, element_matrix, projectors, coupling, connectivity, send_list, atom_of_cell):
    fe_count = lax.axis_size("fe")
    v, conn, send = wavefunctions, connectivity, send_list.reshape(1, GHOST)
    pot, couple = potential.reshape(1, NODES), coupling.T
    ups, downs = call(
        first_kernel,
        [((40, 640), F32), ((24, 384), F32)],
        [VM, VM, VM, SM, VM, VM, VM],
        v, conn, send, atom_of_cell, projectors, pot, couple,
    )
    up, down = shifted(ups, 1), shifted(downs, -1)
    maps, pn, pt = call(
        local_kernel,
        [((8, NODES), jnp.int32), ((4 * SLOT, NODES), F32), ((2, NODES, LANES), BF16)],
        [VM] * 3,
        conn, send, projectors,
    )
    (e,) = call(split_kernel, [((2, NPC, NPC), BF16)], [VM], element_matrix)

    def inner(mode, v, previous):
        outs = [((BANDS, NODES), F32)] * (2 if mode == "last" else 1)
        return call(functools.partial(inner_kernel, mode), outs, [VM] * 6, v, previous, conn, maps, pot, e)

    previous = current = v
    (base,) = inner("first", current, previous)
    p, pe, k, index = call(
        joined_kernel,
        [((2, 256, NODES), BF16), ((2, NPC, LANES), BF16), ((512, 256), BF16), ((8, NODES), jnp.int32)],
        [VM, VM, VM, SM, VM, VM, VM],
        up, down, maps, atom_of_cell, projectors, couple, pn,
    )
    shared = (conn, index, e, p, pe, k)
    messages = [((BANDS, 640), F32), ((BANDS, 384), F32), ((BANDS, 640), F32), ((BANDS, 640), F32)]
    for step in range(DEGREE):
        last = step == DEGREE - 1
        kernel = functools.partial(outer_kernel, step > 0, (1.0 if step == 0 else 2.0) / HALF_WIDTH)
        vectors = ((BANDS, NODES), F32)
        given = (base, ups, downs, up, down, *shared)
        if last:
            copied = ((lax.axis_size("band"), BANDS, NODES), F32)
            new, copied = call(kernel, [vectors, copied], [VM] * 11, *given)
            everyone = lax.all_to_all(copied, "band", 0, 0).reshape(-1, NODES)
            ups, downs, one, two = call(pack_kernel, messages, [VM] * 4, new, conn, send, pt)
        else:
            new, ups, downs, one, two = call(kernel, [vectors] + messages, [VM] * 13, *given, send, pt)
        previous, current = current, new
        up, down = swapped(one, 1), swapped(two, 0)
        base, *result = inner("last" if last else "middle", current, current if last else previous)
    (copies,) = call(
        gram_kernel,
        [((8, 32, LANES), F32)],
        [VM] * 12 + [pl.BlockSpec(memory_space=pl.ANY)],
        base, ups, downs, up, down, *shared, current, everyone,
        scratch=[pltpu.VMEM((LANES, NODES), F32), pltpu.SemaphoreType.DMA],
    )
    near = [[8 * i + j for j in range(8)] for i in range(fe_count // 8)]
    far = [[8 * i + j for i in range(fe_count // 8)] for j in range(8)]
    parts = lax.all_to_all(copies, "fe", 0, 0, axis_index_groups=near)
    (copies,) = call(add_kernel, [((fe_count // 8, 32, LANES), F32)], [VM], parts)
    parts = lax.all_to_all(copies, "fe", 0, 0, axis_index_groups=far)
    projected, correlation = call(
        functools.partial(last_kernel, 1.0 / (NODES * fe_count)),
        [((BANDS, LANES), F32), ((BANDS, LANES), F32)],
        [VM],
        parts,
    )
    return result[0], projected.T, correlation.T


def solution(mesh):
    in_specs = (
        P("band", "fe"),
        P("fe"),
        P(),
        P("fe", None, None),
        P(),
        P("fe", None),
        P("fe"),
        P("fe"),
    )
    out_specs = (P("band", "fe"), P(None, "band"), P(None, "band"))
    return jax.shard_map(on_device, mesh=mesh, in_specs=in_specs, out_specs=out_specs, check_vma=False)
```
